32 devices in a mesh: groups: 2 (over x), ctx: 16 (over z, y, core).
Axes of the slice: x: 2, y: 2, z: 4, core: 2. Of those that a mesh axis runs over, the one named last changes fastest.
Arguments:
- features: bfloat16 [64, 16, 24, 192], P(('groups', 'ctx')), parts along dimension 0, may hold values from -6 to 6
- clip_ids: int32 [64], P('groups'), parts along dimension 0, may hold values from 0 to 7, never falling along the last dimension, each value on 1 to 8 neighbouring positions
- gain_first: float32 [192], replicated, may hold values from 0.1 to 1.9
- weight_first: bfloat16 [27, 192, 192], P(None, None, 'ctx'), may hold values from -0.078125 to 0.078125
- gain_second: float32 [192], replicated, may hold values from 0.1 to 1.9
- weight_second: bfloat16 [27, 192, 192], P(None, None, 'ctx'), may hold values from -0.078125 to 0.078125
- gain_third: float32 [192], replicated, may hold values from 0.1 to 1.9
- weight_out: bfloat16 [27, 192, 16], replicated, may hold values from -0.078125 to 0.078125
- embed_weight: bfloat16 [64, 3072], replicated, may hold values from -0.75 to 0.75
- shift_mod: float32 [3072], replicated, may hold values from -3 to 3
- scale_mod: float32 [3072], replicated, may hold values from -0.5 to 0.5
- token_order: int32 [6144], P(('groups', 'ctx')), parts along dimension 0, may hold values from 0 to 3071, each once
Outputs:
- tokens_out: bfloat16 [6144, 3072], P(('groups', 'ctx')), parts along dimension 0
The draws below stay inside these ranges and needn't reach their ends.
There are 2 independent parts, one for each index of `groups`. The reference program is written for one: setup_inputs(seed, part) draws one part's arguments, and reference() takes and returns one part's arrays. A program takes and returns all parts, laid end to end along the dimension named above; an argument that names none is the same for every part. Nothing has to cross between parts.
Inputs may be any that keep to these rules, and one draw needn't show every extreme that they name: `clip_ids`: clip ids never fall along the frames and start at 0; each clip spans 1 to 8 frames, and some clip spans exactly 8. `token_order`: each patch index appears exactly once.
All inputs are finite; a program needn't handle non-finite values.
Results may differ from the reference program's by a relative error of at most 0.014.
Values may be sent and summed in bfloat16 or wider, within the bound.
No kernel may reach another device: no remote copies, remote signals or barrier semaphores. Data moves between devices by JAX's collectives and lax.ppermute only.
A program may use at most 128 MiB of HBM per device.

```python
import math
import jax
import jax.numpy as jnp
import numpy as np
from jax import lax

C = 192
CZ = 16
D = 3072
HB = 16
WB = 24
FRAMES = 32
TOKENS = 3072


def block_scale(own_key, extent, pieces, smallest, high):
    gain, own = 1.0, jax.random.fold_in(own_key, 6)
    for dim, shards_of in pieces:
        draws = jnp.exp(jax.random.uniform(jax.random.fold_in(own, dim), (shards_of,), jnp.float32, smallest / len(pieces), high / len(pieces)))
        gain = gain * jnp.repeat(draws, extent[dim] // shards_of).reshape([-1 if axis == dim else 1 for axis in range(len(extent))])
    return gain


def length_profile(count, total, reach, skew):
    loads = [(1 << 20) // math.isqrt(standing ** skew) + 1 for standing in range(2, count + 1)]
    spare, counts = total - reach - (count - 1), [1] * (count - 1)
    while spare > 0:
        candidates = [i for i in range(count - 1) if counts[i] < reach]
        whole, budget = sum([loads[i] for i in candidates]), spare
        for i in candidates:
            extra = min(reach - counts[i], max(1, budget * loads[i] // whole), spare)
            counts[i] = counts[i] + extra
            spare = spare - extra
    return np.array([reach] + counts)


def uneven(own_key, amount, total, bound, slope):
    if amount == 2:
        one = jax.random.randint(own_key, (), max(1, total - bound), min(bound, total - 1) + 1)
        return jnp.stack([one, total - one])
    lengths = jnp.asarray(length_profile(amount, total, bound, slope), jnp.int32)
    couples = (amount - 1) // 2
    donor, taker = lengths[1:1 + 2 * couples:2], lengths[2:2 + 2 * couples:2]
    room = jnp.minimum(donor - 1, bound - taker)
    moved = jax.random.randint(jax.random.fold_in(own_key, 1), (couples,), 0, 1 << 20) % (room + 1)
    lengths = lengths.at[1:1 + 2 * couples:2].set(donor - moved).at[2:2 + 2 * couples:2].set(taker + moved)
    return lengths[jax.random.permutation(jax.random.fold_in(own_key, 2), amount)]


def normal_values(rng, dims, scale, bound, cuts=(), held_as=jnp.bfloat16):
    level = block_scale(rng, dims, cuts, -0.22, 0.18) if cuts else 1.0
    entries = jax.random.normal(rng, dims, jnp.float32) * scale * level
    return jnp.minimum(jnp.maximum(entries, -bound), bound).astype(held_as)


def setup_inputs(seed: int = 0, part: int = 0) -> dict:
    keys = jax.random.split(jax.random.key(seed), 13)
    own_keys = jax.random.split(jax.random.fold_in(keys[12], part), 13)
    return {
        "features": normal_values(own_keys[0], (FRAMES, HB, WB, C), 1.0, 6.0, ((0, 16),)),
        "clip_ids": jnp.searchsorted(jnp.cumsum(uneven(own_keys[1], FRAMES // 4, FRAMES, 8, 2)), jnp.arange(FRAMES), side="right").astype(jnp.int32),
        "gain_first": jnp.clip(1.0 + 0.18 * jax.random.normal(keys[2], (C,), jnp.float32), 0.1, 1.9),
        "weight_first": normal_values(keys[3], (27, C, C), (27 * C) ** -0.5, 0.078125, ((2, 16),)),
        "gain_second": jnp.clip(1.0 + 0.18 * jax.random.normal(keys[4], (C,), jnp.float32), 0.1, 1.9),
        "weight_second": normal_values(keys[5], (27, C, C), (27 * C) ** -0.5, 0.078125, ((2, 16),)),
        "gain_third": jnp.clip(1.0 + 0.18 * jax.random.normal(keys[6], (C,), jnp.float32), 0.1, 1.9),
        "weight_out": normal_values(keys[7], (27, C, CZ), (27 * C) ** -0.5, 0.078125),
        "embed_weight": normal_values(keys[8], (4 * CZ, D), (4 * CZ) ** -0.5, 0.75),
        "shift_mod": normal_values(keys[9], (D,), 0.5, 3.0, (), jnp.float32),
        "scale_mod": jnp.clip(jax.random.uniform(keys[10], (D,), jnp.float32, -0.5, 0.5), -0.5, 0.5),
        "token_order": jax.random.permutation(own_keys[11], TOKENS).astype(jnp.int32),
    }


def earlier_frames(values, clip_ids, steps_back):
    if steps_back == 0:
        return values
    length = values.shape[0]
    moved_back = jnp.concatenate([jnp.zeros((steps_back,) + values.shape[1:], values.dtype), values[:length - steps_back]], axis=0)
    moved_ids = jnp.concatenate([jnp.full((steps_back,), -1, jnp.int32), clip_ids[:length - steps_back].astype(jnp.int32)])
    same_clip = moved_ids == clip_ids.astype(jnp.int32)
    return jnp.where(same_clip[:, None, None, None], moved_back, jnp.zeros((), values.dtype))

def causal_conv(values, clip_ids, weight):
    frames, height, breadth, channels = values.shape
    summed = jnp.zeros((frames * height * breadth, weight.shape[2]), jnp.float32)
    for frame_tap in range(3):
        source = earlier_frames(values, clip_ids, 2 - frame_tap)
        padded = jnp.pad(source, ((0, 0), (1, 1), (1, 1), (0, 0)))
        for row_tap in range(3):
            for col_tap in range(3):
                shifted = padded[:, row_tap:row_tap + height, col_tap:col_tap + breadth, :].reshape(-1, channels)
                summed = summed + jnp.dot(shifted, weight[frame_tap * 9 + row_tap * 3 + col_tap], preferred_element_type=jnp.float32)
    return summed.reshape(frames, height, breadth, weight.shape[2])

def rms_silu(values, gain_vector):
    values = values.astype(jnp.float32)
    normed = values * lax.rsqrt(lax.optimization_barrier(jnp.mean(values * values, axis=-1, keepdims=True)) + 1e-06) * gain_vector.astype(jnp.float32)
    return jax.nn.silu(normed).astype(jnp.bfloat16)

def to_patches(latents):
    frames, height, breadth, latent_depth = latents.shape
    grid = latents.reshape(frames, height // 2, 2, breadth // 2, 2, latent_depth).transpose(0, 1, 3, 2, 4, 5)
    return grid.reshape(frames * (height // 2) * (breadth // 2), 4 * latent_depth)

def modulate(ordered, embed_weight, shift_mod, scale_mod):
    embedded = jnp.dot(ordered, embed_weight, preferred_element_type=jnp.float32)
    center = lax.optimization_barrier(jnp.mean(embedded, axis=-1, keepdims=True))
    centered = embedded - center
    variance = lax.optimization_barrier(jnp.mean(centered * centered, axis=-1, keepdims=True))
    normed = centered * lax.rsqrt(variance + 1e-06)
    return (normed * (1.0 + scale_mod.astype(jnp.float32)) + shift_mod.astype(jnp.float32)).astype(jnp.bfloat16)

def reference(features, clip_ids, gain_first, weight_first, gain_second, weight_second, gain_third, weight_out, embed_weight, shift_mod, scale_mod, token_order):
    first_in = rms_silu(features, gain_first)
    first_out = causal_conv(first_in, clip_ids, weight_first).astype(jnp.bfloat16)
    second_in = rms_silu(first_out, gain_second)
    block_out = (features.astype(jnp.float32) + causal_conv(second_in, clip_ids, weight_second)).astype(jnp.bfloat16)
    head_in = rms_silu(block_out, gain_third)
    latents = causal_conv(head_in, clip_ids, weight_out).astype(jnp.bfloat16)
    patches = to_patches(latents)
    ordered = patches[token_order.astype(jnp.int32)]
    return modulate(ordered, embed_weight, shift_mod, scale_mod)
```

```python
import functools

import jax
import jax.numpy as jnp
from jax import lax
from jax.experimental import pallas as pl
from jax.experimental.pallas import tpu as pltpu
from jax.sharding import PartitionSpec as P

LANES = 128
SUBLANES = 8
UNIT_ROWS = 256
SCRATCH_ROWS = 288
NT = (((1,), (1,)), ((), ()))
VMEM_SPEC = pl.BlockSpec(memory_space=pltpu.VMEM)
SMEM_SPEC = pl.BlockSpec(memory_space=pltpu.SMEM)
PARAMS = pltpu.CompilerParams(vmem_limit_bytes=56 * 2**20)


def xor_permute(value, axis, mask):
    count = lax.axis_size(axis)
    return lax.ppermute(value, axis, [(source, source ^ mask) for source in range(count)])


def to_next(value, axis):
    count = lax.axis_size(axis)
    return lax.ppermute(value, axis, [(source, source + 1) for source in range(count - 1)])


def unit_geometry(taps, unit_channels):
    pairs = (taps + 1) // 2
    head_rows = -(-unit_channels * taps // SUBLANES) * SUBLANES
    return pairs, head_rows


def pack_kernel(half_ref, *refs, unit_channels):
    count = len(refs) // 2
    staged = refs[-1]
    for weight_ref, unit_ref in zip(refs[:count], refs[count:-1]):
        _, taps, channels = weight_ref.shape
        pairs, head_rows = unit_geometry(taps, unit_channels)
        tail = channels - LANES
        staged[...] = jnp.zeros_like(staged)
        for channel in range(unit_channels):
            rows = weight_ref[half_ref[0] * unit_channels + channel].astype(jnp.float32)
            staged[channel * taps : channel * taps + taps, :] = rows[:, :LANES]
            at = head_rows + channel * pairs
            staged[at : at + pairs, 0:tail] = rows[:pairs, LANES:]
            staged[at : at + taps - pairs, tail : 2 * tail] = rows[pairs:, LANES:]
        unit_ref[...] = staged[...].astype(jnp.bfloat16)


def pack_units(half, weights, unit_channels):
    return pl.pallas_call(
        functools.partial(pack_kernel, unit_channels=unit_channels),
        out_shape=[jax.ShapeDtypeStruct((UNIT_ROWS, LANES), jnp.bfloat16)] * len(weights),
        in_specs=[SMEM_SPEC] + [VMEM_SPEC] * len(weights),
        out_specs=[VMEM_SPEC] * len(weights),
        scratch_shapes=[pltpu.VMEM((UNIT_ROWS, LANES), jnp.float32)],
        compiler_params=PARAMS,
    )(half, *weights)


def pack_whole(weight, units):
    outputs, taps, channels = weight.shape
    unit_channels = outputs // units
    pairs, head_rows = unit_geometry(taps, unit_channels)
    split = weight.reshape(units, unit_channels, taps, channels)
    head = split[..., :LANES].reshape(units, unit_channels * taps, LANES)
    head = jnp.pad(head, ((0, 0), (0, head_rows - unit_channels * taps), (0, 0)))
    low, high = split[:, :, :pairs, LANES:], split[:, :, pairs:, LANES:]
    high = jnp.pad(high, ((0, 0), (0, 0), (0, 2 * pairs - taps), (0, 0)))
    tail = jnp.concatenate([low, high], axis=-1).reshape(units, unit_channels * pairs, LANES)
    both = jnp.concatenate([head, tail], axis=1)
    return jnp.pad(both, ((0, 0), (0, UNIT_ROWS - both.shape[1]), (0, 0)))


def expand_kernel(weight_ref, wide_ref):
    depth, channels = weight_ref.shape[1:]
    wide_ref[...] = jnp.zeros_like(wide_ref)
    for u in range(4):
        for v in range(4):
            for a in range(3):
                for r in range(2):
                    for s in range(2):
                        if 0 <= u - r <= 2 and 0 <= v - s <= 2:
                            at = ((a * 2 + r) * 2 + s) * depth
                            wide_ref[4 * u + v, at : at + depth, :channels] = weight_ref[
                                9 * a + 3 * (u - r) + (v - s)
                            ]


def expand_weight_out(weight):
    _, depth, channels = weight.shape
    return pl.pallas_call(
        expand_kernel,
        out_shape=jax.ShapeDtypeStruct((16, 12 * depth, 2 * LANES), jnp.bfloat16),
        in_specs=[VMEM_SPEC],
        out_specs=VMEM_SPEC,
        compiler_params=PARAMS,
    )(weight)


def rms_silu(values, gain_vector):
    normed = (
        values * lax.rsqrt(jnp.mean(values * values, axis=-1, keepdims=True) + 1e-06) * gain_vector
    )
    return jax.nn.silu(normed)


def same_clip(clips_ref, frame, steps_back):
    earlier = jnp.maximum(frame - steps_back, 0)
    return (frame >= steps_back) & (clips_ref[earlier] == clips_ref[frame])


def split_lanes(values):
    tail = values[:, LANES:]
    fill = jnp.zeros((values.shape[0], 2 * LANES - values.shape[1]), values.dtype)
    return values[:, :LANES], jnp.concatenate([tail, fill], axis=1)


def place_frame(values, at, head_x, low_x, high_x):
    breadth, height = head_x.shape[2] - 2, head_x.shape[3]
    row = lax.broadcasted_iota(jnp.int32, (values.shape[0], LANES), 0) % height
    head, tail = split_lanes(values)
    count = values.shape[0]
    for tap in range(3):
        for part, part_x in ((head, head_x), (tail, low_x)):
            if tap == 0:
                part = jnp.where(row == 0, 0.0, pltpu.roll(part, 1, 0))
            if tap == 2:
                part = jnp.where(row == height - 1, 0.0, pltpu.roll(part, count - 1, 0))
            part_x[tap, at, 1 : breadth + 1] = part.reshape(breadth, height, LANES).astype(
                jnp.bfloat16
            )
            if part_x is low_x:
                high_x[tap, at, 1 : breadth + 1] = (
                    pltpu.roll(part, LANES // 2, 1).reshape(breadth, height, LANES)
                ).astype(jnp.bfloat16)


def clear_rims(arrays):
    for array in arrays:
        frames, wide = array.shape[1], array.shape[2]
        array[:, frames - 1] = jnp.zeros_like(array[:, frames - 1])
        array[:, :, 0] = jnp.zeros_like(array[:, :, 0])
        array[:, :, wide - 1] = jnp.zeros_like(array[:, :, wide - 1])


def unpack_units(unit_refs, rhs, staged, taps, unit_channels):
    pairs, head_rows = unit_geometry(taps, unit_channels)
    staged[:, UNIT_ROWS:] = jnp.zeros_like(staged[:, UNIT_ROWS:])
    done = 0
    for unit_ref in unit_refs:
        couples = unit_ref.shape[0] // 2

        def couple_step(couple, carry, unit_ref=unit_ref, done=done):
            for one in range(2):
                staged[one, :UNIT_ROWS] = unit_ref[2 * couple + one].astype(jnp.float32)
            to = pl.ds(pl.multiple_of((done + couple) * 16, 16), 16)
            for tap in range(taps):
                rows = [staged[one, pl.ds(tap, 8, stride=taps), :] for one in range(2)]
                rhs[tap, to, :] = jnp.concatenate(rows, axis=0).astype(jnp.bfloat16)
            for pair in range(pairs):
                rows = [staged[one, pl.ds(head_rows + pair, 8, stride=pairs), :] for one in range(2)]
                rhs[taps + pair, to, :] = jnp.concatenate(rows, axis=0).astype(jnp.bfloat16)
            return carry

        lax.fori_loop(0, couples, couple_step, 0)
        done += couples


def convolve(clips_ref, first, head_x, low_x, high_x, rhs, frames, taps):
    zero_frame = head_x.shape[1] - 1
    breadth, height = head_x.shape[2] - 2, head_x.shape[3]
    pairs = (taps + 1) // 2
    source = [
        [
            jnp.where(same_clip(clips_ref, first + frame, 2 - tap), frame + tap, zero_frame)
            for tap in range(3)
        ]
        for frame in range(frames)
    ]

    def shifted(array, tap):
        a, b, e = tap // 9, tap // 3 % 3, tap % 3
        return jnp.concatenate(
            [
                array[b, source[frame][a], e : e + breadth].reshape(breadth * height, LANES)
                for frame in range(frames)
            ],
            axis=0,
        )

    def chunk(index):
        if index < taps:
            return shifted(head_x, index)
        pair = index - taps
        low = shifted(low_x, pair)
        return low + shifted(high_x, pair + pairs) if pair + pairs < taps else low

    total = taps + pairs
    summed = None
    for begin in range(0, total, 14):
        end = min(begin + 14, total)
        part = lax.dot_general(
            jnp.concatenate([chunk(index) for index in range(begin, end)], axis=1),
            jnp.concatenate([rhs[index] for index in range(begin, end)], axis=1),
            NT,
            preferred_element_type=jnp.float32,
        )
        summed = part if summed is None else summed + part
    return summed


def first_kernel(
    clips_ref, first_ref, own_ref, rim_ref, gain_first_ref, gain_second_ref, pick_ref, *rest,
    taps, unit_channels,
):
    *unit_refs, out_ref, head_x, low_x, high_x, rhs, staged = rest
    frames, breadth, height, channels = own_ref.shape
    clear_rims((head_x, low_x, high_x))
    for frame in range(frames + 2):
        values = rim_ref[frame] if frame < 2 else own_ref[frame - 2]
        values = values.astype(jnp.float32).reshape(breadth * height, channels)
        place_frame(rms_silu(values, gain_first_ref[...]), frame, head_x, low_x, high_x)
    unpack_units(unit_refs, rhs, staged, taps, unit_channels)
    summed = convolve(clips_ref, first_ref[0], head_x, low_x, high_x, rhs, frames, taps)
    first_out = jnp.dot(
        summed.astype(jnp.bfloat16), pick_ref[...], preferred_element_type=jnp.float32
    )
    out_ref[...] = (
        rms_silu(first_out, gain_second_ref[...])
        .astype(jnp.bfloat16)
        .reshape(frames, breadth, height, channels)
    )


def second_kernel(
    clips_ref, first_ref, own_ref, rim_ref, features_ref, gain_ref, pick_ref, wide_ref, *rest,
    taps, unit_channels,
):
    *unit_refs, own_out, next_out, head_x, low_x, high_x, rhs, staged, plain, windows = rest
    frames, breadth, height, channels = own_ref.shape
    pixels = breadth * height
    rows, columns = height // 2, breadth // 2
    width = wide_ref.shape[1] // 3
    first = first_ref[0]
    clear_rims((head_x, low_x, high_x))
    for frame in range(frames + 2):
        values = rim_ref[frame] if frame < 2 else own_ref[frame - 2]
        values = values.astype(jnp.float32).reshape(pixels, channels)
        place_frame(values, frame, head_x, low_x, high_x)
    unpack_units(unit_refs, rhs, staged, taps, unit_channels)
    summed = convolve(clips_ref, first, head_x, low_x, high_x, rhs, frames, taps)
    features = lax.dot_general(
        features_ref[...].reshape(frames * pixels, channels),
        pick_ref[...],
        NT,
        preferred_element_type=jnp.float32,
    )
    block_out = jnp.dot(
        (features + summed).astype(jnp.bfloat16), pick_ref[...], preferred_element_type=jnp.float32
    )
    head_in = rms_silu(block_out, gain_ref[...])
    for part, values in enumerate(split_lanes(head_in)):
        plain[part] = values
    windows[...] = jnp.zeros_like(windows)
    half = frames * pixels // 2
    row = lax.broadcasted_iota(jnp.int32, (half, LANES), 0) % rows
    for part in range(2):
        even = plain[part, pl.ds(0, half, stride=2), :]
        odd = plain[part, pl.ds(1, half, stride=2), :]
        before = jnp.where(row == 0, 0.0, pltpu.roll(odd, 1, 0))
        after = jnp.where(row == rows - 1, 0.0, pltpu.roll(even, half - 1, 0))
        for u, values in enumerate((before, even, odd, after)):
            windows[u, part, :, 1 : breadth + 1] = values.reshape(frames, breadth, rows, LANES)
    chunks = []
    for u in range(4):
        for v in range(4):
            for part in range(2):
                chunks.append(
                    jnp.concatenate(
                        [
                            windows[u, part, frame, pl.ds(v, columns, stride=2)].reshape(
                                columns * rows, LANES
                            )
                            for frame in range(frames)
                        ],
                        axis=0,
                    ).astype(jnp.bfloat16)
                )
    outs = lax.dot_general(
        jnp.concatenate(chunks, axis=1),
        jnp.concatenate([wide_ref[window] for window in range(16)], axis=1),
        NT,
        preferred_element_type=jnp.float32,
    )
    spots = columns * rows

    def from_frame(frame, tap):
        return outs[frame * spots : (frame + 1) * spots, tap * width : (tap + 1) * width]

    def gathered(frame, sources):
        total = jnp.zeros((spots, width), jnp.float32)
        for tap in range(3):
            source = frame + tap - 2
            if source in sources:
                kept = same_clip(clips_ref, jnp.minimum(first + frame, clips_ref.shape[0] - 1), 2 - tap)
                total = total + jnp.where(kept, from_frame(source, tap), 0.0)
        return total

    own = range(frames)
    own_out[...] = jnp.concatenate([gathered(frame, own) for frame in own], axis=1)
    next_out[...] = jnp.concatenate(
        [gathered(frame + frames, own) for frame in own], axis=1
    )


def conv_scratch(frames, breadth, height, taps, outputs):
    pairs = (taps + 1) // 2
    image = pltpu.VMEM((3, frames + 3, breadth + 2, height, LANES), jnp.bfloat16)
    return [image] * 3 + [
        pltpu.VMEM((taps + pairs, outputs, LANES), jnp.bfloat16),
        pltpu.VMEM((2, SCRATCH_ROWS, LANES), jnp.float32),
    ]


def embed_kernel(
    spot_ref, lane_ref, embed_ref, scale_ref, shift_ref, *rest
):
    *patch_refs, out_ref = rest
    width = embed_ref.shape[0]
    total = jnp.zeros((out_ref.shape[0], LANES), jnp.float32)
    begin = 0
    for patch_ref in patch_refs:
        count = patch_ref.shape[0]
        spots = lax.broadcasted_iota(jnp.int32, (out_ref.shape[0], count), 1) + begin
        chosen = jnp.where(spots == spot_ref[...], 1.0, 0.0).astype(jnp.bfloat16)
        total = total + jnp.dot(chosen, patch_ref[...], preferred_element_type=jnp.float32)
        begin += count
    turned = pltpu.roll(total, width, 1)
    ordered = jnp.where(lane_ref[...] == 0, total, turned)[:, :width].astype(jnp.bfloat16)
    embedded = jnp.dot(ordered, embed_ref[...], preferred_element_type=jnp.float32)
    center = jnp.mean(embedded, axis=-1, keepdims=True)
    centered = embedded - center
    variance = jnp.mean(centered * centered, axis=-1, keepdims=True)
    normed = centered * lax.rsqrt(variance + 1e-06)
    out_ref[...] = (normed * (1.0 + scale_ref[...]) + shift_ref[...]).astype(out_ref.dtype)


def gather_units(unit):
    line = jnp.stack([unit] + [xor_permute(unit, "ctx", 4 * step) for step in (1, 2, 3)])
    across = xor_permute(line, "ctx", 2)
    other = xor_permute(line, "groups", 1)
    corner_low = xor_permute(other[:2], "ctx", 2)
    corner_high = xor_permute(across[2:], "groups", 1)
    chip = jnp.concatenate([line, across, other, corner_low, corner_high])
    return [chip, xor_permute(chip, "ctx", 1)]


def unit_channel_map(grid, group, device, unit_channels, units):
    unit = jnp.arange(units * SUBLANES, dtype=jnp.int32) // SUBLANES
    within = jnp.arange(units * SUBLANES, dtype=jnp.int32) % SUBLANES
    if grid:
        step, kind, core = unit % 4, unit // 4 % 4, unit // 16
        source = device ^ (4 * step + 2 * (kind % 2) + core)
        unit = source * 2 + (group ^ (kind // 2))
    return jnp.where(within < unit_channels, unit * unit_channels + within, -1)


def body(
    features,
    clip_ids,
    gain_first,
    weight_first,
    gain_second,
    weight_second,
    gain_third,
    weight_out,
    embed_weight,
    shift_mod,
    scale_mod,
    token_order,
):
    frames, height, breadth, channels = features.shape
    taps = weight_first.shape[0]
    groups, devices = lax.axis_size("groups"), lax.axis_size("ctx")
    group, device = lax.axis_index("groups"), lax.axis_index("ctx")
    grid = groups == 2 and devices == 16
    units = 32
    unit_channels = channels // units

    by_output = [weight.transpose(2, 0, 1) for weight in (weight_first, weight_second)]
    if grid:
        half = group.astype(jnp.int32).reshape(1)
        packed = pack_units(half, by_output, unit_channels)
        units_first, units_second = [gather_units(unit) for unit in packed]
    else:
        units_first, units_second = [
            [pack_whole(lax.all_gather(weight, "ctx", axis=0, tiled=True), units)]
            for weight in by_output
        ]
    channel_map = unit_channel_map(grid, group, device, unit_channels, units)
    pick = (channel_map[:, None] == jnp.arange(channels, dtype=jnp.int32)).astype(jnp.bfloat16)
    wide = expand_weight_out(weight_out.transpose(0, 2, 1))

    first = (device * frames).astype(jnp.int32).reshape(1)
    turned = features.transpose(0, 2, 1, 3)
    scratch = conv_scratch(frames, breadth, height, taps, units * SUBLANES)
    image = jax.ShapeDtypeStruct((frames, breadth, height, channels), jnp.bfloat16)
    second_in = pl.pallas_call(
        functools.partial(first_kernel, taps=taps, unit_channels=unit_channels),
        out_shape=image,
        in_specs=[SMEM_SPEC] * 2 + [VMEM_SPEC] * (5 + len(units_first)),
        out_specs=VMEM_SPEC,
        scratch_shapes=scratch,
        compiler_params=PARAMS,
    )(
        clip_ids, first, turned, to_next(turned[frames - 2 :], "ctx"), gain_first.reshape(1, -1),
        gain_second.reshape(1, -1), pick, *units_first,
    )

    depth = weight_out.shape[2]
    spots = (height // 2) * (breadth // 2)
    partial = jax.ShapeDtypeStruct((spots, frames * 4 * depth), jnp.float32)
    own_part, next_part = pl.pallas_call(
        functools.partial(second_kernel, taps=taps, unit_channels=unit_channels),
        out_shape=[partial, partial],
        in_specs=[SMEM_SPEC] * 2 + [VMEM_SPEC] * (6 + len(units_second)),
        out_specs=[VMEM_SPEC] * 2,
        scratch_shapes=scratch
        + [
            pltpu.VMEM((2, frames * breadth * height, LANES), jnp.float32),
            pltpu.VMEM((4, 2, frames, breadth + 2, height // 2, LANES), jnp.float32),
        ],
        compiler_params=PARAMS,
    )(
        clip_ids, first, second_in, to_next(second_in[frames - 2 :], "ctx"), turned,
        gain_third.reshape(1, -1), pick, wide, *units_second,
    )
    patches = (own_part + to_next(next_part, "ctx")).astype(jnp.bfloat16)

    frame, spot = token_order // spots, token_order % spots
    spot = spot % (breadth // 2) * (height // 2) + spot // (breadth // 2)
    owner = frame // frames
    if grid:
        line = jnp.concatenate([patches] + [xor_permute(patches, "ctx", 4 * k) for k in (1, 2, 3)])
        sheet = jnp.concatenate([line, xor_permute(line, "ctx", 2)])
        pieces = [sheet, xor_permute(sheet, "ctx", 1)]
        away = owner ^ device
        place = (away % 2 * 2 + away // 2 % 2) * 4 + away // 4
    else:
        pieces = [lax.all_gather(patches, "ctx", axis=0, tiled=True)]
        place = owner
    spot = (place * spots + spot).reshape(-1, 1)
    lane = (frame % frames).reshape(-1, 1)

    tokens, width = token_order.shape[0], embed_weight.shape[1]
    block = 48 if tokens % 48 == 0 else tokens
    column = pl.BlockSpec((block, 1), lambda i: (i, 0))
    row = pl.BlockSpec((1, width), lambda i: (0, 0))
    return pl.pallas_call(
        embed_kernel,
        out_shape=jax.ShapeDtypeStruct((tokens, width), jnp.bfloat16),
        grid=(tokens // block,),
        in_specs=[column, column, pl.BlockSpec(embed_weight.shape, lambda i: (0, 0)), row, row]
        + [pl.BlockSpec(piece.shape, lambda i: (0, 0)) for piece in pieces],
        out_specs=pl.BlockSpec((block, width), lambda i: (i, 0)),
        compiler_params=PARAMS,
    )(
        spot, lane, embed_weight, scale_mod.reshape(1, -1), shift_mod.reshape(1, -1), *pieces
    )


def solution(mesh):
    in_specs = (
        P(("groups", "ctx"), None, None, None),
        P("groups"),
        P(),
        P(None, None, "ctx"),
        P(),
        P(None, None, "ctx"),
        P(),
        P(),
        P(),
        P(),
        P(),
        P(("groups", "ctx")),
    )
    out_specs = P(("groups", "ctx"), None)
    return jax.shard_map(body, mesh=mesh, in_specs=in_specs, out_specs=out_specs, check_vma=False)
```

```python
import functools

import jax
import jax.numpy as jnp
from jax import lax
from jax.experimental import pallas as pl
from jax.experimental.pallas import tpu as pltpu
from jax.sharding import PartitionSpec as P

LANES = 128
SUBLANES = 8
UNIT_ROWS = 256
SCRATCH_ROWS = 288
NT = (((1,), (1,)), ((), ()))
VMEM_SPEC = pl.BlockSpec(memory_space=pltpu.VMEM)
SMEM_SPEC = pl.BlockSpec(memory_space=pltpu.SMEM)
PARAMS = pltpu.CompilerParams(vmem_limit_bytes=56 * 2**20)


def xor_permute(value, axis, mask):
    count = lax.axis_size(axis)
    return lax.ppermute(value, axis, [(source, source ^ mask) for source in range(count)])


def to_next(value, axis):
    count = lax.axis_size(axis)
    return lax.ppermute(value, axis, [(source, source + 1) for source in range(count - 1)])


def unit_geometry(taps, unit_channels):
    pairs = (taps + 1) // 2
    head_rows = -(-unit_channels * taps // SUBLANES) * SUBLANES
    return pairs, head_rows


def pack_kernel(half_ref, *refs, unit_channels):
    count = len(refs) // 2
    staged = refs[-1]
    for weight_ref, unit_ref in zip(refs[:count], refs[count:-1]):
        _, taps, channels = weight_ref.shape
        pairs, head_rows = unit_geometry(taps, unit_channels)
        tail = channels - LANES
        staged[...] = jnp.zeros_like(staged)
        for channel in range(unit_channels):
            rows = weight_ref[half_ref[0] * unit_channels + channel].astype(jnp.float32)
            staged[channel * taps : channel * taps + taps, :] = rows[:, :LANES]
            at = head_rows + channel * pairs
            staged[at : at + pairs, 0:tail] = rows[:pairs, LANES:]
            staged[at : at + taps - pairs, tail : 2 * tail] = rows[pairs:, LANES:]
        unit_ref[...] = staged[...].astype(jnp.bfloat16)


def pack_units(half, weights, unit_channels):
    return pl.pallas_call(
        functools.partial(pack_kernel, unit_channels=unit_channels),
        out_shape=[jax.ShapeDtypeStruct((UNIT_ROWS, LANES), jnp.bfloat16)] * len(weights),
        in_specs=[SMEM_SPEC] + [VMEM_SPEC] * len(weights),
        out_specs=[VMEM_SPEC] * len(weights),
        scratch_shapes=[pltpu.VMEM((UNIT_ROWS, LANES), jnp.float32)],
        compiler_params=PARAMS,
    )(half, *weights)


def pack_whole(weight, units):
    outputs, taps, channels = weight.shape
    unit_channels = outputs // units
    pairs, head_rows = unit_geometry(taps, unit_channels)
    split = weight.reshape(units, unit_channels, taps, channels)
    head = split[..., :LANES].reshape(units, unit_channels * taps, LANES)
    head = jnp.pad(head, ((0, 0), (0, head_rows - unit_channels * taps), (0, 0)))
    low, high = split[:, :, :pairs, LANES:], split[:, :, pairs:, LANES:]
    high = jnp.pad(high, ((0, 0), (0, 0), (0, 2 * pairs - taps), (0, 0)))
    tail = jnp.concatenate([low, high], axis=-1).reshape(units, unit_channels * pairs, LANES)
    both = jnp.concatenate([head, tail], axis=1)
    return jnp.pad(both, ((0, 0), (0, UNIT_ROWS - both.shape[1]), (0, 0)))


def expand_kernel(weight_ref, wide_ref):
    depth, channels = weight_ref.shape[1:]
    wide_ref[...] = jnp.zeros_like(wide_ref)
    for u in range(4):
        for v in range(4):
            for a in range(3):
                for r in range(2):
                    for s in range(2):
                        if 0 <= u - r <= 2 and 0 <= v - s <= 2:
                            at = ((a * 2 + r) * 2 + s) * depth
                            wide_ref[4 * u + v, at : at + depth, :channels] = weight_ref[
                                9 * a + 3 * (u - r) + (v - s)
                            ]


def expand_weight_out(weight):
    _, depth, channels = weight.shape
    return pl.pallas_call(
        expand_kernel,
        out_shape=jax.ShapeDtypeStruct((16, 12 * depth, 2 * LANES), jnp.bfloat16),
        in_specs=[VMEM_SPEC],
        out_specs=VMEM_SPEC,
        compiler_params=PARAMS,
    )(weight)


def rms_silu(values, gain_vector):
    normed = (
        values * lax.rsqrt(jnp.mean(values * values, axis=-1, keepdims=True) + 1e-06) * gain_vector
    )
    return jax.nn.silu(normed)


def same_clip(clips_ref, frame, steps_back):
    earlier = jnp.maximum(frame - steps_back, 0)
    return (frame >= steps_back) & (clips_ref[earlier] == clips_ref[frame])


def split_lanes(values):
    tail = values[:, LANES:]
    fill = jnp.zeros((values.shape[0], 2 * LANES - values.shape[1]), values.dtype)
    return values[:, :LANES], jnp.concatenate([tail, fill], axis=1)


def place_frame(values, at, head_x, low_x, high_x):
    breadth, height = head_x.shape[2] - 2, head_x.shape[3]
    row = lax.broadcasted_iota(jnp.int32, (values.shape[0], LANES), 0) % height
    head, tail = split_lanes(values)
    count = values.shape[0]
    for tap in range(3):
        for part, part_x in ((head, head_x), (tail, low_x)):
            if tap == 0:
                part = jnp.where(row == 0, 0.0, pltpu.roll(part, 1, 0))
            if tap == 2:
                part = jnp.where(row == height - 1, 0.0, pltpu.roll(part, count - 1, 0))
            part_x[tap, at, 1 : breadth + 1] = part.reshape(breadth, height, LANES).astype(
                jnp.bfloat16
            )
            if part_x is low_x:
                high_x[tap, at, 1 : breadth + 1] = (
                    pltpu.roll(part, LANES // 2, 1).reshape(breadth, height, LANES)
                ).astype(jnp.bfloat16)


def clear_rims(arrays):
    for array in arrays:
        frames, wide = array.shape[1], array.shape[2]
        array[:, frames - 1] = jnp.zeros_like(array[:, frames - 1])
        array[:, :, 0] = jnp.zeros_like(array[:, :, 0])
        array[:, :, wide - 1] = jnp.zeros_like(array[:, :, wide - 1])


def unpack_units(unit_refs, rhs, staged, taps, unit_channels):
    pairs, head_rows = unit_geometry(taps, unit_channels)
    staged[:, UNIT_ROWS:] = jnp.zeros_like(staged[:, UNIT_ROWS:])
    done = 0
    for unit_ref in unit_refs:
        couples = unit_ref.shape[0] // 2

        def couple_step(couple, carry, unit_ref=unit_ref, done=done):
            for one in range(2):
                staged[one, :UNIT_ROWS] = unit_ref[2 * couple + one].astype(jnp.float32)
            to = pl.ds(pl.multiple_of((done + couple) * 16, 16), 16)
            for tap in range(taps):
                rows = [staged[one, pl.ds(tap, 8, stride=taps), :] for one in range(2)]
                rhs[tap, to, :] = jnp.concatenate(rows, axis=0).astype(jnp.bfloat16)
            for pair in range(pairs):
                rows = [staged[one, pl.ds(head_rows + pair, 8, stride=pairs), :] for one in range(2)]
                rhs[taps + pair, to, :] = jnp.concatenate(rows, axis=0).astype(jnp.bfloat16)
            return carry

        lax.fori_loop(0, couples, couple_step, 0)
        done += couples


def convolve(clips_ref, first, head_x, low_x, high_x, rhs, frames, taps):
    zero_frame = head_x.shape[1] - 1
    breadth, height = head_x.shape[2] - 2, head_x.shape[3]
    pairs = (taps + 1) // 2
    source = [
        [
            jnp.where(same_clip(clips_ref, first + frame, 2 - tap), frame + tap, zero_frame)
            for tap in range(3)
        ]
        for frame in range(frames)
    ]

    def shifted(array, tap):
        a, b, e = tap // 9, tap // 3 % 3, tap % 3
        return jnp.concatenate(
            [
                array[b, source[frame][a], e : e + breadth].reshape(breadth * height, LANES)
                for frame in range(frames)
            ],
            axis=0,
        )

    def chunk(index):
        if index < taps:
            return shifted(head_x, index)
        pair = index - taps
        low = shifted(low_x, pair)
        return low + shifted(high_x, pair + pairs) if pair + pairs < taps else low

    total = taps + pairs
    summed = None
    for begin in range(0, total, 14):
        end = min(begin + 14, total)
        part = lax.dot_general(
            jnp.concatenate([chunk(index) for index in range(begin, end)], axis=1),
            jnp.concatenate([rhs[index] for index in range(begin, end)], axis=1),
            NT,
            preferred_element_type=jnp.float32,
        )
        summed = part if summed is None else summed + part
    return summed


def first_kernel(
    clips_ref, first_ref, own_ref, rim_ref, gain_first_ref, gain_second_ref, pick_ref, *rest,
    taps, unit_channels,
):
    *unit_refs, out_ref, head_x, low_x, high_x, rhs, staged = rest
    frames, breadth, height, channels = own_ref.shape
    clear_rims((head_x, low_x, high_x))
    for frame in range(frames + 2):
        values = rim_ref[frame] if frame < 2 else own_ref[frame - 2]
        values = values.astype(jnp.float32).reshape(breadth * height, channels)
        place_frame(rms_silu(values, gain_first_ref[...]), frame, head_x, low_x, high_x)
    unpack_units(unit_refs, rhs, staged, taps, unit_channels)
    summed = convolve(clips_ref, first_ref[0], head_x, low_x, high_x, rhs, frames, taps)
    first_out = jnp.dot(
        summed.astype(jnp.bfloat16), pick_ref[...], preferred_element_type=jnp.float32
    )
    out_ref[...] = (
        rms_silu(first_out, gain_second_ref[...])
        .astype(jnp.bfloat16)
        .reshape(frames, breadth, height, channels)
    )


def second_kernel(
    clips_ref, first_ref, own_ref, rim_ref, features_ref, gain_ref, pick_ref, wide_ref, *rest,
    taps, unit_channels,
):
    *unit_refs, parts_out, head_x, low_x, high_x, rhs, staged, plain, windows = rest
    frames, breadth, height, channels = own_ref.shape
    pixels = breadth * height
    rows, columns = height // 2, breadth // 2
    width = wide_ref.shape[1] // 3
    first = first_ref[0]
    clear_rims((head_x, low_x, high_x))
    for frame in range(frames + 2):
        values = rim_ref[frame] if frame < 2 else own_ref[frame - 2]
        values = values.astype(jnp.float32).reshape(pixels, channels)
        place_frame(values, frame, head_x, low_x, high_x)
    unpack_units(unit_refs, rhs, staged, taps, unit_channels)
    summed = convolve(clips_ref, first, head_x, low_x, high_x, rhs, frames, taps)
    features = lax.dot_general(
        features_ref[...].reshape(frames * pixels, channels),
        pick_ref[...],
        NT,
        preferred_element_type=jnp.float32,
    )
    block_out = jnp.dot(
        (features + summed).astype(jnp.bfloat16), pick_ref[...], preferred_element_type=jnp.float32
    )
    head_in = rms_silu(block_out, gain_ref[...])
    for part, values in enumerate(split_lanes(head_in)):
        plain[part] = values
    windows[...] = jnp.zeros_like(windows)
    half = frames * pixels // 2
    row = lax.broadcasted_iota(jnp.int32, (half, LANES), 0) % rows
    for part in range(2):
        even = plain[part, pl.ds(0, half, stride=2), :]
        odd = plain[part, pl.ds(1, half, stride=2), :]
        before = jnp.where(row == 0, 0.0, pltpu.roll(odd, 1, 0))
        after = jnp.where(row == rows - 1, 0.0, pltpu.roll(even, half - 1, 0))
        for u, values in enumerate((before, even, odd, after)):
            windows[u, part, :, 1 : breadth + 1] = values.reshape(frames, breadth, rows, LANES)
    chunks = []
    for u in range(4):
        for v in range(4):
            for part in range(2):
                chunks.append(
                    jnp.concatenate(
                        [
                            windows[u, part, frame, pl.ds(v, columns, stride=2)].reshape(
                                columns * rows, LANES
                            )
                            for frame in range(frames)
                        ],
                        axis=0,
                    ).astype(jnp.bfloat16)
                )
    outs = lax.dot_general(
        jnp.concatenate(chunks, axis=1),
        jnp.concatenate([wide_ref[window] for window in range(16)], axis=1),
        NT,
        preferred_element_type=jnp.float32,
    )
    spots = columns * rows

    def from_frame(frame, tap):
        return outs[frame * spots : (frame + 1) * spots, tap * width : (tap + 1) * width]

    def gathered(frame, sources):
        total = jnp.zeros((spots, width), jnp.float32)
        for tap in range(3):
            source = frame + tap - 2
            if source in sources:
                kept = same_clip(clips_ref, jnp.minimum(first + frame, clips_ref.shape[0] - 1), 2 - tap)
                total = total + jnp.where(kept, from_frame(source, tap), 0.0)
        return total

    own = range(frames)
    parts = [
        jnp.concatenate([gathered(frame + ahead, own) for frame in own], axis=1)
        for ahead in (0, frames)
    ]
    parts_out[...] = jnp.concatenate(parts, axis=0).astype(jnp.bfloat16)


def conv_scratch(frames, breadth, height, taps, outputs):
    pairs = (taps + 1) // 2
    image = pltpu.VMEM((3, frames + 3, breadth + 2, height, LANES), jnp.bfloat16)
    return [image] * 3 + [
        pltpu.VMEM((taps + pairs, outputs, LANES), jnp.bfloat16),
        pltpu.VMEM((2, SCRATCH_ROWS, LANES), jnp.float32),
    ]


def embed_kernel(place_ref, embed_ref, scale_ref, shift_ref, *rest):
    *patch_refs, out_ref = rest
    width = embed_ref.shape[0]
    tokens = out_ref.shape[0]
    total = jnp.zeros((tokens, LANES), jnp.float32)
    begin = 0
    for patch_ref in patch_refs:
        count = patch_ref.shape[0]
        spots = lax.broadcasted_iota(jnp.int32, (tokens, count), 1) + begin
        chosen = (spots == place_ref[:, 0:1]) | (spots == place_ref[:, 1:2])
        chosen = jnp.where(chosen, 1.0, 0.0).astype(jnp.bfloat16)
        total = total + jnp.dot(chosen, patch_ref[...], preferred_element_type=jnp.float32)
        begin += count
    turned = pltpu.roll(total, width, 1)
    ordered = jnp.where(place_ref[:, 2:3] == 0, total, turned)[:, :width].astype(jnp.bfloat16)
    embedded = jnp.dot(ordered, embed_ref[...], preferred_element_type=jnp.float32)
    center = jnp.mean(embedded, axis=-1, keepdims=True)
    centered = embedded - center
    variance = jnp.mean(centered * centered, axis=-1, keepdims=True)
    normed = centered * lax.rsqrt(variance + 1e-06)
    out_ref[...] = (normed * (1.0 + scale_ref[...]) + shift_ref[...]).astype(out_ref.dtype)


def along_line(unit):
    return jnp.stack([unit] + [xor_permute(unit, "ctx", 4 * step) for step in (1, 2, 3)])


def round_square(line):
    return xor_permute(line, "ctx", 2), xor_permute(line, "groups", 1)


def whole_chip(line, across, other):
    corner_low = xor_permute(other[:2], "ctx", 2)
    corner_high = xor_permute(across[2:], "groups", 1)
    chip = jnp.concatenate([line, across, other, corner_low, corner_high])
    return [chip, xor_permute(chip, "ctx", 1)]


def unit_channel_map(grid, group, device, unit_channels, units):
    unit = jnp.arange(units * SUBLANES, dtype=jnp.int32) // SUBLANES
    within = jnp.arange(units * SUBLANES, dtype=jnp.int32) % SUBLANES
    if grid:
        step, kind, core = unit % 4, unit // 4 % 4, unit // 16
        source = device ^ (4 * step + 2 * (kind % 2) + core)
        unit = source * 2 + (group ^ (kind // 2))
    return jnp.where(within < unit_channels, unit * unit_channels + within, -1)


def body(
    features,
    clip_ids,
    gain_first,
    weight_first,
    gain_second,
    weight_second,
    gain_third,
    weight_out,
    embed_weight,
    shift_mod,
    scale_mod,
    token_order,
):
    frames, height, breadth, channels = features.shape
    taps = weight_first.shape[0]
    groups, devices = lax.axis_size("groups"), lax.axis_size("ctx")
    group, device = lax.axis_index("groups"), lax.axis_index("ctx")
    grid = groups == 2 and devices == 16
    units = 32
    unit_channels = channels // units

    by_output = [weight.transpose(2, 0, 1) for weight in (weight_first, weight_second)]
    channel_map = unit_channel_map(grid, group, device, unit_channels, units)
    pick = (channel_map[:, None] == jnp.arange(channels, dtype=jnp.int32)).astype(jnp.bfloat16)
    wide = expand_weight_out(weight_out.transpose(0, 2, 1))
    turned = features.transpose(0, 2, 1, 3)
    turned_rim = to_next(turned[frames - 2 :], "ctx")

    spots = (height // 2) * (breadth // 2)
    frame, spot = token_order // spots, token_order % spots
    spot = spot % (breadth // 2) * (height // 2) + spot // (breadth // 2)
    owner = frame // frames

    def piece_of(source):
        if not grid:
            return source
        away = source ^ device
        return (away % 2 * 2 + away // 2 % 2) * 4 + away // 4

    own_place = piece_of(owner) * 2 * spots + spot
    sent_place = jnp.where(owner > 0, (piece_of(jnp.maximum(owner - 1, 0)) * 2 + 1) * spots + spot, -1)
    place = jnp.stack([own_place, sent_place, frame % frames], axis=1)

    if grid:
        half = group.astype(jnp.int32).reshape(1)
        packed_first, packed_second = pack_units(half, by_output, unit_channels)
        line_first = along_line(packed_first)
        line_first, wide, pick, place = lax.optimization_barrier((line_first, wide, pick, place))
        square_first = round_square(line_first)
        line_second = along_line(packed_second)
        line_second, square_first, turned_rim = lax.optimization_barrier(
            (line_second, square_first, turned_rim)
        )
        units_first = whole_chip(line_first, *square_first)
        units_second = whole_chip(line_second, *round_square(line_second))
    else:
        units_first, units_second = [
            [pack_whole(lax.all_gather(weight, "ctx", axis=0, tiled=True), units)]
            for weight in by_output
        ]

    first = (device * frames).astype(jnp.int32).reshape(1)
    scratch = conv_scratch(frames, breadth, height, taps, units * SUBLANES)
    image = jax.ShapeDtypeStruct((frames, breadth, height, channels), jnp.bfloat16)
    second_in = pl.pallas_call(
        functools.partial(first_kernel, taps=taps, unit_channels=unit_channels),
        out_shape=image,
        in_specs=[SMEM_SPEC] * 2 + [VMEM_SPEC] * (5 + len(units_first)),
        out_specs=VMEM_SPEC,
        scratch_shapes=scratch,
        compiler_params=PARAMS,
    )(
        clip_ids, first, turned, turned_rim, gain_first.reshape(1, -1),
        gain_second.reshape(1, -1), pick, *units_first,
    )

    depth = weight_out.shape[2]
    parts = pl.pallas_call(
        functools.partial(second_kernel, taps=taps, unit_channels=unit_channels),
        out_shape=jax.ShapeDtypeStruct((2 * spots, frames * 4 * depth), jnp.bfloat16),
        in_specs=[SMEM_SPEC] * 2 + [VMEM_SPEC] * (6 + len(units_second)),
        out_specs=VMEM_SPEC,
        scratch_shapes=scratch
        + [
            pltpu.VMEM((2, frames * breadth * height, LANES), jnp.float32),
            pltpu.VMEM((4, 2, frames, breadth + 2, height // 2, LANES), jnp.float32),
        ],
        compiler_params=PARAMS,
    )(
        clip_ids, first, second_in, to_next(second_in[frames - 2 :], "ctx"), turned,
        gain_third.reshape(1, -1), pick, wide, *units_second,
    )
    if grid:
        line = jnp.concatenate([parts] + [xor_permute(parts, "ctx", 4 * k) for k in (1, 2, 3)])
        sheet = jnp.concatenate([line, xor_permute(line, "ctx", 2)])
        pieces = [sheet, xor_permute(sheet, "ctx", 1)]
    else:
        pieces = [lax.all_gather(parts, "ctx", axis=0, tiled=True)]

    tokens, width = token_order.shape[0], embed_weight.shape[1]
    return pl.pallas_call(
        embed_kernel,
        out_shape=jax.ShapeDtypeStruct((tokens, width), jnp.bfloat16),
        in_specs=[VMEM_SPEC] * (4 + len(pieces)),
        out_specs=VMEM_SPEC,
        compiler_params=PARAMS,
    )(
        place, embed_weight, scale_mod.reshape(1, -1), shift_mod.reshape(1, -1), *pieces
    )


def solution(mesh):
    in_specs = (
        P(("groups", "ctx"), None, None, None),
        P("groups"),
        P(),
        P(None, None, "ctx"),
        P(),
        P(None, None, "ctx"),
        P(),
        P(),
        P(),
        P(),
        P(),
        P(("groups", "ctx")),
    )
    out_specs = P(("groups", "ctx"), None)
    return jax.shard_map(body, mesh=mesh, in_specs=in_specs, out_specs=out_specs, check_vma=False)
```

```python
import functools

import jax
import jax.numpy as jnp
from jax import lax
from jax.experimental import pallas as pl
from jax.experimental.pallas import tpu as pltpu
from jax.sharding import PartitionSpec as P

LANES = 128
SUBLANES = 8
UNIT_ROWS = 256
SCRATCH_ROWS = 288
NT = (((1,), (1,)), ((), ()))
TN = (((0,), (0,)), ((), ()))
VMEM_SPEC = pl.BlockSpec(memory_space=pltpu.VMEM)
SMEM_SPEC = pl.BlockSpec(memory_space=pltpu.SMEM)
IN_VMEM = functools.partial(pltpu.with_memory_space_constraint, memory_space=pltpu.VMEM)
PARAMS = pltpu.CompilerParams(vmem_limit_bytes=56 * 2**20)


def xor_permute(value, axis, mask):
    count = lax.axis_size(axis)
    return lax.ppermute(value, axis, [(source, source ^ mask) for source in range(count)])


def to_next(value, axis):
    count = lax.axis_size(axis)
    return lax.ppermute(value, axis, [(source, source + 1) for source in range(count - 1)])


def unit_geometry(taps, unit_channels):
    pairs = (taps + 1) // 2
    head_rows = -(-unit_channels * taps // SUBLANES) * SUBLANES
    return pairs, head_rows


def pack_kernel(half_ref, *refs, unit_channels):
    count = len(refs) // 2
    staged = refs[-1]
    for weight_ref, unit_ref in zip(refs[:count], refs[count:-1]):
        _, taps, channels = weight_ref.shape
        pairs, head_rows = unit_geometry(taps, unit_channels)
        tail = channels - LANES
        staged[...] = jnp.zeros_like(staged)
        for channel in range(unit_channels):
            rows = weight_ref[half_ref[0] * unit_channels + channel].astype(jnp.float32)
            staged[channel * taps : channel * taps + taps, :] = rows[:, :LANES]
            at = head_rows + channel * pairs
            staged[at : at + pairs, 0:tail] = rows[:pairs, LANES:]
            staged[at : at + taps - pairs, tail : 2 * tail] = rows[pairs:, LANES:]
        unit_ref[...] = staged[...].astype(jnp.bfloat16)


def pack_units(half, weights, unit_channels):
    return pl.pallas_call(
        functools.partial(pack_kernel, unit_channels=unit_channels),
        out_shape=[pltpu.VMEM((UNIT_ROWS, LANES), jnp.bfloat16)] * len(weights),
        in_specs=[SMEM_SPEC] + [VMEM_SPEC] * len(weights),
        out_specs=[VMEM_SPEC] * len(weights),
        scratch_shapes=[pltpu.VMEM((UNIT_ROWS, LANES), jnp.float32)],
        compiler_params=PARAMS,
    )(half, *weights)


def pack_whole(weight, units):
    outputs, taps, channels = weight.shape
    unit_channels = outputs // units
    pairs, head_rows = unit_geometry(taps, unit_channels)
    split = weight.reshape(units, unit_channels, taps, channels)
    head = split[..., :LANES].reshape(units, unit_channels * taps, LANES)
    head = jnp.pad(head, ((0, 0), (0, head_rows - unit_channels * taps), (0, 0)))
    low, high = split[:, :, :pairs, LANES:], split[:, :, pairs:, LANES:]
    high = jnp.pad(high, ((0, 0), (0, 0), (0, 2 * pairs - taps), (0, 0)))
    tail = jnp.concatenate([low, high], axis=-1).reshape(units, unit_channels * pairs, LANES)
    both = jnp.concatenate([head, tail], axis=1)
    return jnp.pad(both, ((0, 0), (0, UNIT_ROWS - both.shape[1]), (0, 0)))


def expand_kernel(weight_ref, wide_ref):
    depth, channels = weight_ref.shape[1:]
    wide_ref[...] = jnp.zeros_like(wide_ref)
    for u in range(4):
        for v in range(4):
            for a in range(3):
                for r in range(2):
                    for s in range(2):
                        if 0 <= u - r <= 2 and 0 <= v - s <= 2:
                            at = ((a * 2 + r) * 2 + s) * depth
                            wide_ref[4 * u + v, at : at + depth, :channels] = weight_ref[
                                9 * a + 3 * (u - r) + (v - s)
                            ]


def expand_weight_out(weight):
    _, depth, channels = weight.shape
    return pl.pallas_call(
        expand_kernel,
        out_shape=pltpu.VMEM((16, 12 * depth, 2 * LANES), jnp.bfloat16),
        in_specs=[VMEM_SPEC],
        out_specs=VMEM_SPEC,
        compiler_params=PARAMS,
    )(weight)


def rms_silu(values, gain_vector):
    normed = (
        values * lax.rsqrt(jnp.mean(values * values, axis=-1, keepdims=True) + 1e-06) * gain_vector
    )
    return jax.nn.silu(normed)


def same_clip(clips_ref, frame, steps_back):
    earlier = jnp.maximum(frame - steps_back, 0)
    return (frame >= steps_back) & (clips_ref[earlier] == clips_ref[frame])


def split_lanes(values):
    tail = values[:, LANES:]
    fill = jnp.zeros((values.shape[0], 2 * LANES - values.shape[1]), values.dtype)
    return values[:, :LANES], jnp.concatenate([tail, fill], axis=1)


def place_frame(values, at, head_x, low_x, high_x):
    breadth, height = head_x.shape[2] - 2, head_x.shape[3]
    row = lax.broadcasted_iota(jnp.int32, (values.shape[0], LANES), 0) % height
    head, tail = split_lanes(values)
    count = values.shape[0]
    for tap in range(3):
        for part, part_x in ((head, head_x), (tail, low_x)):
            if tap == 0:
                part = jnp.where(row == 0, 0.0, pltpu.roll(part, 1, 0))
            if tap == 2:
                part = jnp.where(row == height - 1, 0.0, pltpu.roll(part, count - 1, 0))
            part_x[tap, at, 1 : breadth + 1] = part.reshape(breadth, height, LANES).astype(
                jnp.bfloat16
            )
            if part_x is low_x:
                high_x[tap, at, 1 : breadth + 1] = (
                    pltpu.roll(part, LANES // 2, 1).reshape(breadth, height, LANES)
                ).astype(jnp.bfloat16)


def clear_rims(arrays):
    for array in arrays:
        frames, wide = array.shape[1], array.shape[2]
        array[:, frames - 1] = jnp.zeros_like(array[:, frames - 1])
        array[:, :, 0] = jnp.zeros_like(array[:, :, 0])
        array[:, :, wide - 1] = jnp.zeros_like(array[:, :, wide - 1])


def unpack_units(unit_refs, rhs, staged, taps, unit_channels):
    pairs, head_rows = unit_geometry(taps, unit_channels)
    staged[:, UNIT_ROWS:] = jnp.zeros_like(staged[:, UNIT_ROWS:])
    done = 0
    for unit_ref in unit_refs:
        couples = unit_ref.shape[0] // 2

        def couple_step(couple, carry, unit_ref=unit_ref, done=done):
            for one in range(2):
                staged[one, :UNIT_ROWS] = unit_ref[2 * couple + one].astype(jnp.float32)
            to = pl.ds(pl.multiple_of((done + couple) * 16, 16), 16)
            for tap in range(taps):
                rows = [staged[one, pl.ds(tap, 8, stride=taps), :] for one in range(2)]
                rhs[tap, to, :] = jnp.concatenate(rows, axis=0).astype(jnp.bfloat16)
            for pair in range(pairs):
                rows = [staged[one, pl.ds(head_rows + pair, 8, stride=pairs), :] for one in range(2)]
                rhs[taps + pair, to, :] = jnp.concatenate(rows, axis=0).astype(jnp.bfloat16)
            return carry

        lax.fori_loop(0, couples, couple_step, 0)
        done += couples


def convolve(clips_ref, first, head_x, low_x, high_x, rhs, frames, taps):
    zero_frame = head_x.shape[1] - 1
    breadth, height = head_x.shape[2] - 2, head_x.shape[3]
    pairs = (taps + 1) // 2
    source = [
        [
            jnp.where(same_clip(clips_ref, first + frame, 2 - tap), frame + tap, zero_frame)
            for tap in range(3)
        ]
        for frame in range(frames)
    ]

    def shifted(array, tap):
        a, b, e = tap // 9, tap // 3 % 3, tap % 3
        return jnp.concatenate(
            [
                array[b, source[frame][a], e : e + breadth].reshape(breadth * height, LANES)
                for frame in range(frames)
            ],
            axis=0,
        )

    def chunk(index):
        if index < taps:
            return shifted(head_x, index)
        pair = index - taps
        low = shifted(low_x, pair)
        return low + shifted(high_x, pair + pairs) if pair + pairs < taps else low

    total = taps + pairs
    summed = None
    for begin in range(0, total, 14):
        end = min(begin + 14, total)
        part = lax.dot_general(
            jnp.concatenate([chunk(index) for index in range(begin, end)], axis=1),
            jnp.concatenate([rhs[index] for index in range(begin, end)], axis=1),
            NT,
            preferred_element_type=jnp.float32,
        )
        summed = part if summed is None else summed + part
    return summed


def first_kernel(
    clips_ref, first_ref, own_ref, rim_ref, gain_first_ref, gain_second_ref, pick_ref, *rest,
    taps, unit_channels,
):
    *unit_refs, out_ref, head_x, low_x, high_x, rhs, staged = rest
    frames, breadth, height, channels = own_ref.shape
    clear_rims((head_x, low_x, high_x))
    for frame in range(frames + 2):
        values = rim_ref[frame] if frame < 2 else own_ref[frame - 2]
        values = values.astype(jnp.float32).reshape(breadth * height, channels)
        place_frame(rms_silu(values, gain_first_ref[...]), frame, head_x, low_x, high_x)
    unpack_units(unit_refs, rhs, staged, taps, unit_channels)
    summed = convolve(clips_ref, first_ref[0], head_x, low_x, high_x, rhs, frames, taps)
    first_out = jnp.dot(
        summed.astype(jnp.bfloat16), pick_ref[...], preferred_element_type=jnp.float32
    )
    out_ref[...] = (
        rms_silu(first_out, gain_second_ref[...])
        .astype(jnp.bfloat16)
        .reshape(frames, breadth, height, channels)
    )


def second_kernel(
    clips_ref, first_ref, own_ref, rim_ref, features_ref, gain_ref, pick_ref, wide_ref, *rest,
    taps, unit_channels,
):
    *unit_refs, parts_out, head_x, low_x, high_x, rhs, staged, plain, windows = rest
    frames, breadth, height, channels = own_ref.shape
    pixels = breadth * height
    rows, columns = height // 2, breadth // 2
    width = wide_ref.shape[1] // 3
    first = first_ref[0]
    clear_rims((head_x, low_x, high_x))
    for frame in range(frames + 2):
        values = rim_ref[frame] if frame < 2 else own_ref[frame - 2]
        values = values.astype(jnp.float32).reshape(pixels, channels)
        place_frame(values, frame, head_x, low_x, high_x)
    unpack_units(unit_refs, rhs, staged, taps, unit_channels)
    summed = convolve(clips_ref, first, head_x, low_x, high_x, rhs, frames, taps)
    features = lax.dot_general(
        features_ref[...].reshape(frames * pixels, channels),
        pick_ref[...],
        NT,
        preferred_element_type=jnp.float32,
    )
    block_out = jnp.dot(
        (features + summed).astype(jnp.bfloat16), pick_ref[...], preferred_element_type=jnp.float32
    )
    head_in = rms_silu(block_out, gain_ref[...])
    for part, values in enumerate(split_lanes(head_in)):
        plain[part] = values
    windows[...] = jnp.zeros_like(windows)
    half = frames * pixels // 2
    row = lax.broadcasted_iota(jnp.int32, (half, LANES), 0) % rows
    for part in range(2):
        even = plain[part, pl.ds(0, half, stride=2), :]
        odd = plain[part, pl.ds(1, half, stride=2), :]
        before = jnp.where(row == 0, 0.0, pltpu.roll(odd, 1, 0))
        after = jnp.where(row == rows - 1, 0.0, pltpu.roll(even, half - 1, 0))
        for u, values in enumerate((before, even, odd, after)):
            windows[u, part, :, 1 : breadth + 1] = values.reshape(frames, breadth, rows, LANES)
    chunks = []
    for u in range(4):
        for v in range(4):
            for part in range(2):
                chunks.append(
                    jnp.concatenate(
                        [
                            windows[u, part, frame, pl.ds(v, columns, stride=2)].reshape(
                                columns * rows, LANES
                            )
                            for frame in range(frames)
                        ],
                        axis=0,
                    ).astype(jnp.bfloat16)
                )
    outs = lax.dot_general(
        jnp.concatenate(chunks, axis=1),
        jnp.concatenate([wide_ref[window] for window in range(16)], axis=1),
        NT,
        preferred_element_type=jnp.float32,
    )
    spots = columns * rows

    def from_frame(frame, tap):
        return outs[frame * spots : (frame + 1) * spots, tap * width : (tap + 1) * width]

    def gathered(frame, sources):
        total = jnp.zeros((spots, width), jnp.float32)
        for tap in range(3):
            source = frame + tap - 2
            if source in sources:
                kept = same_clip(clips_ref, jnp.minimum(first + frame, clips_ref.shape[0] - 1), 2 - tap)
                total = total + jnp.where(kept, from_frame(source, tap), 0.0)
        return total

    own = range(frames)
    parts = [
        jnp.concatenate([gathered(frame + ahead, own) for frame in own], axis=1)
        for ahead in (0, frames)
    ]
    parts_out[...] = jnp.concatenate(parts, axis=0).astype(jnp.bfloat16)


def conv_scratch(frames, breadth, height, taps, outputs):
    pairs = (taps + 1) // 2
    image = pltpu.VMEM((3, frames + 3, breadth + 2, height, LANES), jnp.bfloat16)
    return [image] * 3 + [
        pltpu.VMEM((taps + pairs, outputs, LANES), jnp.bfloat16),
        pltpu.VMEM((2, SCRATCH_ROWS, LANES), jnp.float32),
    ]


def embed_kernel(place_ref, embed_ref, scale_ref, shift_ref, *rest):
    *patch_refs, out_ref = rest
    width = embed_ref.shape[0]
    tokens = out_ref.shape[0]
    total = jnp.zeros((LANES, tokens), jnp.float32)
    begin = 0
    for patch_ref in patch_refs:
        count = patch_ref.shape[0]
        spots = lax.broadcasted_iota(jnp.int32, (count, tokens), 0) + begin
        chosen = (spots == place_ref[0:1, :]) | (spots == place_ref[1:2, :])
        chosen = jnp.where(chosen, 1.0, 0.0).astype(jnp.bfloat16)
        total = total + lax.dot_general(
            patch_ref[...], chosen, TN, preferred_element_type=jnp.float32
        )
        begin += count
    ordered = jnp.where(place_ref[2:3, :] == 0, total[:width], total[width:]).astype(jnp.bfloat16)
    embedded = lax.dot_general(ordered, embed_ref[...], TN, preferred_element_type=jnp.float32)
    center = jnp.mean(embedded, axis=-1, keepdims=True)
    centered = embedded - center
    variance = jnp.mean(centered * centered, axis=-1, keepdims=True)
    normed = centered * lax.rsqrt(variance + 1e-06)
    out_ref[...] = (normed * (1.0 + scale_ref[...]) + shift_ref[...]).astype(out_ref.dtype)


def along_line(unit):
    return [unit] + [xor_permute(unit, "ctx", 4 * step) for step in (1, 2, 3)]


def round_square(line):
    return xor_permute(line, "ctx", 2), xor_permute(line, "groups", 1)


def to_corner(across, other):
    return xor_permute(other[:2], "ctx", 2), xor_permute(across[2:], "groups", 1)


def both_cores(pieces):
    return list(pieces) + [xor_permute(piece, "ctx", 1) for piece in pieces]


def unit_channel_map(grid, group, device, unit_channels, units):
    unit = jnp.arange(units * SUBLANES, dtype=jnp.int32) // SUBLANES
    within = jnp.arange(units * SUBLANES, dtype=jnp.int32) % SUBLANES
    if grid:
        step, kind, core = unit % 4, unit // 4 % 4, unit // 16
        source = device ^ (4 * step + 2 * (kind % 2) + core)
        unit = source * 2 + (group ^ (kind // 2))
    return jnp.where(within < unit_channels, unit * unit_channels + within, -1)


def body(
    features,
    clip_ids,
    gain_first,
    weight_first,
    gain_second,
    weight_second,
    gain_third,
    weight_out,
    embed_weight,
    shift_mod,
    scale_mod,
    token_order,
):
    frames, height, breadth, channels = features.shape
    taps = weight_first.shape[0]
    groups, devices = lax.axis_size("groups"), lax.axis_size("ctx")
    group, device = lax.axis_index("groups"), lax.axis_index("ctx")
    grid = groups == 2 and devices == 16
    units = 32
    unit_channels = channels // units

    by_output = [weight.transpose(2, 0, 1) for weight in (weight_first, weight_second)]
    channel_map = unit_channel_map(grid, group, device, unit_channels, units)
    pick = (channel_map[:, None] == jnp.arange(channels, dtype=jnp.int32)).astype(jnp.bfloat16)
    wide = expand_weight_out(weight_out.transpose(0, 2, 1))
    turned = features.transpose(0, 2, 1, 3)

    spots = (height // 2) * (breadth // 2)
    frame, spot = token_order // spots, token_order % spots
    spot = spot % (breadth // 2) * (height // 2) + spot // (breadth // 2)
    owner = frame // frames

    def piece_of(source):
        if not grid:
            return source
        away = source ^ device
        return (away % 2 * 2 + away // 2 % 2) * 4 + away // 4

    own_place = piece_of(owner) * 2 * spots + spot
    sent_place = jnp.where(owner > 0, (piece_of(jnp.maximum(owner - 1, 0)) * 2 + 1) * spots + spot, -1)
    place = jnp.stack([own_place, sent_place, frame % frames])

    if grid:
        half = group.astype(jnp.int32).reshape(1)
        packed_first, packed_second = pack_units(half, by_output, unit_channels)
        line_first = along_line(packed_first)
        line_first, wide, pick, place, turned = lax.optimization_barrier(
            (line_first, wide, pick, place, turned)
        )
        line_first = jnp.stack(line_first)
        packed_second, rim_source, line_first = lax.optimization_barrier(
            (packed_second, turned, line_first)
        )
        square_first = round_square(line_first)
        line_second = jnp.stack(along_line(packed_second))
        turned_rim = to_next(rim_source[frames - 2 :], "ctx")
        corner_first = to_corner(*square_first)
        line_second, corner_first, turned_rim = lax.optimization_barrier(
            (line_second, corner_first, turned_rim)
        )
        square_second = round_square(line_second)
        units_first = both_cores((line_first, *square_first, *corner_first))
    else:
        units_first, units_second = [
            [pack_whole(lax.all_gather(weight, "ctx", axis=0, tiled=True), units)]
            for weight in by_output
        ]
        turned_rim = to_next(turned[frames - 2 :], "ctx")

    first = (device * frames).astype(jnp.int32).reshape(1)
    scratch = conv_scratch(frames, breadth, height, taps, units * SUBLANES)
    image = pltpu.VMEM((frames, breadth, height, channels), jnp.bfloat16)
    second_in = pl.pallas_call(
        functools.partial(first_kernel, taps=taps, unit_channels=unit_channels),
        out_shape=image,
        in_specs=[SMEM_SPEC] * 2 + [VMEM_SPEC] * (5 + len(units_first)),
        out_specs=VMEM_SPEC,
        scratch_shapes=scratch,
        compiler_params=PARAMS,
    )(
        clip_ids, first, IN_VMEM(turned), IN_VMEM(turned_rim), gain_first.reshape(1, -1),
        gain_second.reshape(1, -1), IN_VMEM(pick), *map(IN_VMEM, units_first),
    )
    second_rim = to_next(second_in[frames - 2 :], "ctx")
    if grid:
        square_second, second_in = lax.optimization_barrier((square_second, second_in))
        corner_second = to_corner(*square_second)
        units_second = both_cores((line_second, *square_second, *corner_second))

    depth = weight_out.shape[2]
    parts = pl.pallas_call(
        functools.partial(second_kernel, taps=taps, unit_channels=unit_channels),
        out_shape=pltpu.VMEM((2 * spots, frames * 4 * depth), jnp.bfloat16),
        in_specs=[SMEM_SPEC] * 2 + [VMEM_SPEC] * (6 + len(units_second)),
        out_specs=VMEM_SPEC,
        scratch_shapes=scratch
        + [
            pltpu.VMEM((2, frames * breadth * height, LANES), jnp.float32),
            pltpu.VMEM((4, 2, frames, breadth + 2, height // 2, LANES), jnp.float32),
        ],
        compiler_params=PARAMS,
    )(
        clip_ids, first, IN_VMEM(second_in), IN_VMEM(second_rim), IN_VMEM(turned),
        gain_third.reshape(1, -1), IN_VMEM(pick), IN_VMEM(wide), *map(IN_VMEM, units_second),
    )
    if grid:
        line = jnp.concatenate(along_line(parts))
        pieces = both_cores((line, xor_permute(line, "ctx", 2)))
    else:
        pieces = [lax.all_gather(parts, "ctx", axis=0, tiled=True)]

    tokens, width = token_order.shape[0], embed_weight.shape[1]
    return pl.pallas_call(
        embed_kernel,
        out_shape=jax.ShapeDtypeStruct((tokens, width), jnp.bfloat16),
        in_specs=[VMEM_SPEC] * (4 + len(pieces)),
        out_specs=VMEM_SPEC,
        compiler_params=PARAMS,
    )(
        IN_VMEM(place), IN_VMEM(embed_weight), scale_mod.reshape(1, -1), shift_mod.reshape(1, -1),
        *map(IN_VMEM, pieces),
    )


def solution(mesh):
    in_specs = (
        P(("groups", "ctx"), None, None, None),
        P("groups"),
        P(),
        P(None, None, "ctx"),
        P(),
        P(None, None, "ctx"),
        P(),
        P(),
        P(),
        P(),
        P(),
        P(("groups", "ctx")),
    )
    out_specs = P(("groups", "ctx"), None)
    return jax.shard_map(body, mesh=mesh, in_specs=in_specs, out_specs=out_specs, check_vma=False)
```

```python
import functools

import jax
import jax.numpy as jnp
from jax import lax
from jax.experimental import pallas as pl
from jax.experimental.pallas import tpu as pltpu
from jax.sharding import PartitionSpec as P

LANES = 128
SUBLANES = 8
UNIT_ROWS = 256
SCRATCH_ROWS = 288
NT = (((1,), (1,)), ((), ()))
TN = (((0,), (0,)), ((), ()))
VMEM_SPEC = pl.BlockSpec(memory_space=pltpu.VMEM)
SMEM_SPEC = pl.BlockSpec(memory_space=pltpu.SMEM)
IN_VMEM = functools.partial(pltpu.with_memory_space_constraint, memory_space=pltpu.VMEM)
SMALL = pltpu.CompilerParams(vmem_limit_bytes=4 * 2**20)
LARGE = pltpu.CompilerParams(vmem_limit_bytes=24 * 2**20)


def xor_permute(value, axis, mask):
    count = lax.axis_size(axis)
    return lax.ppermute(value, axis, [(source, source ^ mask) for source in range(count)])


def to_next(value, axis):
    count = lax.axis_size(axis)
    return lax.ppermute(value, axis, [(source, source + 1) for source in range(count - 1)])


def unit_geometry(taps, unit_channels):
    pairs = (taps + 1) // 2
    head_rows = -(-unit_channels * taps // SUBLANES) * SUBLANES
    return pairs, head_rows


def pack_kernel(half_ref, *refs, unit_channels):
    count = len(refs) // 2
    staged = refs[-1]
    for weight_ref, unit_ref in zip(refs[:count], refs[count:-1]):
        _, taps, channels = weight_ref.shape
        pairs, head_rows = unit_geometry(taps, unit_channels)
        tail = channels - LANES
        staged[...] = jnp.zeros_like(staged)
        for channel in range(unit_channels):
            rows = weight_ref[half_ref[0] * unit_channels + channel].astype(jnp.float32)
            staged[channel * taps : channel * taps + taps, :] = rows[:, :LANES]
            at = head_rows + channel * pairs
            staged[at : at + pairs, 0:tail] = rows[:pairs, LANES:]
            staged[at : at + taps - pairs, tail : 2 * tail] = rows[pairs:, LANES:]
        unit_ref[...] = staged[...].astype(jnp.bfloat16)


def pack_units(half, weights, unit_channels):
    return pl.pallas_call(
        functools.partial(pack_kernel, unit_channels=unit_channels),
        out_shape=[pltpu.VMEM((UNIT_ROWS, LANES), jnp.bfloat16)] * len(weights),
        in_specs=[SMEM_SPEC] + [VMEM_SPEC] * len(weights),
        out_specs=[VMEM_SPEC] * len(weights),
        scratch_shapes=[pltpu.VMEM((UNIT_ROWS, LANES), jnp.float32)],
        compiler_params=SMALL,
    )(half, *weights)


def pack_whole(weight, units):
    outputs, taps, channels = weight.shape
    unit_channels = outputs // units
    pairs, head_rows = unit_geometry(taps, unit_channels)
    split = weight.reshape(units, unit_channels, taps, channels)
    head = split[..., :LANES].reshape(units, unit_channels * taps, LANES)
    head = jnp.pad(head, ((0, 0), (0, head_rows - unit_channels * taps), (0, 0)))
    low, high = split[:, :, :pairs, LANES:], split[:, :, pairs:, LANES:]
    high = jnp.pad(high, ((0, 0), (0, 0), (0, 2 * pairs - taps), (0, 0)))
    tail = jnp.concatenate([low, high], axis=-1).reshape(units, unit_channels * pairs, LANES)
    both = jnp.concatenate([head, tail], axis=1)
    return jnp.pad(both, ((0, 0), (0, UNIT_ROWS - both.shape[1]), (0, 0)))


def expand_kernel(weight_ref, wide_ref):
    depth, channels = weight_ref.shape[1:]
    wide_ref[...] = jnp.zeros_like(wide_ref)
    for u in range(4):
        for v in range(4):
            for a in range(3):
                for r in range(2):
                    for s in range(2):
                        if 0 <= u - r <= 2 and 0 <= v - s <= 2:
                            at = ((a * 2 + r) * 2 + s) * depth
                            wide_ref[4 * u + v, at : at + depth, :channels] = weight_ref[
                                9 * a + 3 * (u - r) + (v - s)
                            ]


def expand_weight_out(weight):
    _, depth, channels = weight.shape
    return pl.pallas_call(
        expand_kernel,
        out_shape=pltpu.VMEM((16, 12 * depth, 2 * LANES), jnp.bfloat16),
        in_specs=[VMEM_SPEC],
        out_specs=VMEM_SPEC,
        compiler_params=SMALL,
    )(weight)


def rms_silu(values, gain_vector):
    normed = (
        values * lax.rsqrt(jnp.mean(values * values, axis=-1, keepdims=True) + 1e-06) * gain_vector
    )
    return jax.nn.silu(normed)


def same_clip(clips_ref, frame, steps_back):
    earlier = jnp.maximum(frame - steps_back, 0)
    return (frame >= steps_back) & (clips_ref[earlier] == clips_ref[frame])


def split_lanes(values):
    tail = values[:, LANES:]
    fill = jnp.zeros((values.shape[0], 2 * LANES - values.shape[1]), values.dtype)
    return values[:, :LANES], jnp.concatenate([tail, fill], axis=1)


def place_frame(values, at, head_x, low_x, high_x):
    breadth, height = head_x.shape[2] - 2, head_x.shape[3]
    row = lax.broadcasted_iota(jnp.int32, (values.shape[0], LANES), 0) % height
    head, tail = split_lanes(values)
    count = values.shape[0]
    for tap in range(3):
        for part, part_x in ((head, head_x), (tail, low_x)):
            if tap == 0:
                part = jnp.where(row == 0, 0.0, pltpu.roll(part, 1, 0))
            if tap == 2:
                part = jnp.where(row == height - 1, 0.0, pltpu.roll(part, count - 1, 0))
            part_x[tap, at, 1 : breadth + 1] = part.reshape(breadth, height, LANES).astype(
                jnp.bfloat16
            )
            if part_x is low_x:
                high_x[tap, at, 1 : breadth + 1] = (
                    pltpu.roll(part, LANES // 2, 1).reshape(breadth, height, LANES)
                ).astype(jnp.bfloat16)


def clear_rims(arrays):
    for array in arrays:
        frames, wide = array.shape[1], array.shape[2]
        array[:, frames - 1] = jnp.zeros_like(array[:, frames - 1])
        array[:, :, 0] = jnp.zeros_like(array[:, :, 0])
        array[:, :, wide - 1] = jnp.zeros_like(array[:, :, wide - 1])


def unpack_units(unit_refs, rhs, staged, taps, unit_channels):
    pairs, head_rows = unit_geometry(taps, unit_channels)
    staged[:, UNIT_ROWS:] = jnp.zeros_like(staged[:, UNIT_ROWS:])
    done = 0
    for unit_ref in unit_refs:
        couples = unit_ref.shape[0] // 2

        def couple_step(couple, carry, unit_ref=unit_ref, done=done):
            for one in range(2):
                staged[one, :UNIT_ROWS] = unit_ref[2 * couple + one].astype(jnp.float32)
            to = pl.ds(pl.multiple_of((done + couple) * 16, 16), 16)
            for tap in range(taps):
                rows = [staged[one, pl.ds(tap, 8, stride=taps), :] for one in range(2)]
                rhs[tap, to, :] = jnp.concatenate(rows, axis=0).astype(jnp.bfloat16)
            for pair in range(pairs):
                rows = [staged[one, pl.ds(head_rows + pair, 8, stride=pairs), :] for one in range(2)]
                rhs[taps + pair, to, :] = jnp.concatenate(rows, axis=0).astype(jnp.bfloat16)
            return carry

        lax.fori_loop(0, couples, couple_step, 0)
        done += couples


def convolve(clips_ref, first, head_x, low_x, high_x, rhs, frames, taps):
    zero_frame = head_x.shape[1] - 1
    breadth, height = head_x.shape[2] - 2, head_x.shape[3]
    pairs = (taps + 1) // 2
    source = [
        [
            jnp.where(same_clip(clips_ref, first + frame, 2 - tap), frame + tap, zero_frame)
            for tap in range(3)
        ]
        for frame in range(frames)
    ]

    def shifted(array, tap):
        a, b, e = tap // 9, tap // 3 % 3, tap % 3
        return jnp.concatenate(
            [
                array[b, source[frame][a], e : e + breadth].reshape(breadth * height, LANES)
                for frame in range(frames)
            ],
            axis=0,
        )

    def chunk(index):
        if index < taps:
            return shifted(head_x, index)
        pair = index - taps
        low = shifted(low_x, pair)
        return low + shifted(high_x, pair + pairs) if pair + pairs < taps else low

    total = taps + pairs
    summed = None
    for begin in range(0, total, 14):
        end = min(begin + 14, total)
        part = lax.dot_general(
            jnp.concatenate([chunk(index) for index in range(begin, end)], axis=1),
            jnp.concatenate([rhs[index] for index in range(begin, end)], axis=1),
            NT,
            preferred_element_type=jnp.float32,
        )
        summed = part if summed is None else summed + part
    return summed


def first_kernel(
    clips_ref, first_ref, own_ref, rim_ref, gain_first_ref, gain_second_ref, pick_ref, *rest,
    taps, unit_channels,
):
    *unit_refs, out_ref, head_x, low_x, high_x, rhs, staged = rest
    frames, breadth, height, channels = own_ref.shape
    clear_rims((head_x, low_x, high_x))
    for frame in range(frames + 2):
        values = rim_ref[frame] if frame < 2 else own_ref[frame - 2]
        values = values.astype(jnp.float32).reshape(breadth * height, channels)
        place_frame(rms_silu(values, gain_first_ref[...]), frame, head_x, low_x, high_x)
    unpack_units(unit_refs, rhs, staged, taps, unit_channels)
    summed = convolve(clips_ref, first_ref[0], head_x, low_x, high_x, rhs, frames, taps)
    first_out = jnp.dot(
        summed.astype(jnp.bfloat16), pick_ref[...], preferred_element_type=jnp.float32
    )
    out_ref[...] = (
        rms_silu(first_out, gain_second_ref[...])
        .astype(jnp.bfloat16)
        .reshape(frames, breadth, height, channels)
    )


def second_kernel(
    clips_ref, first_ref, own_ref, rim_ref, features_ref, gain_ref, pick_ref, wide_ref, *rest,
    taps, unit_channels,
):
    *unit_refs, parts_out, head_x, low_x, high_x, rhs, staged, plain, windows = rest
    frames, breadth, height, channels = own_ref.shape
    pixels = breadth * height
    rows, columns = height // 2, breadth // 2
    width = wide_ref.shape[1] // 3
    first = first_ref[0]
    clear_rims((head_x, low_x, high_x))
    for frame in range(frames + 2):
        values = rim_ref[frame] if frame < 2 else own_ref[frame - 2]
        values = values.astype(jnp.float32).reshape(pixels, channels)
        place_frame(values, frame, head_x, low_x, high_x)
    unpack_units(unit_refs, rhs, staged, taps, unit_channels)
    summed = convolve(clips_ref, first, head_x, low_x, high_x, rhs, frames, taps)
    features = lax.dot_general(
        features_ref[...].reshape(frames * pixels, channels),
        pick_ref[...],
        NT,
        preferred_element_type=jnp.float32,
    )
    block_out = jnp.dot(
        (features + summed).astype(jnp.bfloat16), pick_ref[...], preferred_element_type=jnp.float32
    )
    head_in = rms_silu(block_out, gain_ref[...])
    for part, values in enumerate(split_lanes(head_in)):
        plain[part] = values
    windows[...] = jnp.zeros_like(windows)
    half = frames * pixels // 2
    row = lax.broadcasted_iota(jnp.int32, (half, LANES), 0) % rows
    for part in range(2):
        even = plain[part, pl.ds(0, half, stride=2), :]
        odd = plain[part, pl.ds(1, half, stride=2), :]
        before = jnp.where(row == 0, 0.0, pltpu.roll(odd, 1, 0))
        after = jnp.where(row == rows - 1, 0.0, pltpu.roll(even, half - 1, 0))
        for u, values in enumerate((before, even, odd, after)):
            windows[u, part, :, 1 : breadth + 1] = values.reshape(frames, breadth, rows, LANES)
    chunks = []
    for u in range(4):
        for v in range(4):
            for part in range(2):
                chunks.append(
                    jnp.concatenate(
                        [
                            windows[u, part, frame, pl.ds(v, columns, stride=2)].reshape(
                                columns * rows, LANES
                            )
                            for frame in range(frames)
                        ],
                        axis=0,
                    ).astype(jnp.bfloat16)
                )
    outs = lax.dot_general(
        jnp.concatenate(chunks, axis=1),
        jnp.concatenate([wide_ref[window] for window in range(16)], axis=1),
        NT,
        preferred_element_type=jnp.float32,
    )
    spots = columns * rows

    def from_frame(frame, tap):
        return outs[frame * spots : (frame + 1) * spots, tap * width : (tap + 1) * width]

    def gathered(frame, sources):
        total = jnp.zeros((spots, width), jnp.float32)
        for tap in range(3):
            source = frame + tap - 2
            if source in sources:
                kept = same_clip(clips_ref, jnp.minimum(first + frame, clips_ref.shape[0] - 1), 2 - tap)
                total = total + jnp.where(kept, from_frame(source, tap), 0.0)
        return total

    own = range(frames)
    parts = [
        jnp.concatenate([gathered(frame + ahead, own) for frame in own], axis=1)
        for ahead in (0, frames)
    ]
    parts_out[...] = jnp.concatenate(parts, axis=0).astype(jnp.bfloat16)


def conv_scratch(frames, breadth, height, taps, outputs):
    pairs = (taps + 1) // 2
    image = pltpu.VMEM((3, frames + 3, breadth + 2, height, LANES), jnp.bfloat16)
    return [image] * 3 + [
        pltpu.VMEM((taps + pairs, outputs, LANES), jnp.bfloat16),
        pltpu.VMEM((2, SCRATCH_ROWS, LANES), jnp.float32),
    ]


def embed_kernel(place_ref, embed_ref, scale_ref, shift_ref, *rest):
    *patch_refs, out_ref = rest
    width = embed_ref.shape[0]
    tokens = out_ref.shape[0]
    total = jnp.zeros((LANES, tokens), jnp.float32)
    begin = 0
    for patch_ref in patch_refs:
        count = patch_ref.shape[0]
        spots = lax.broadcasted_iota(jnp.int32, (count, tokens), 0) + begin
        chosen = (spots == place_ref[0:1, :]) | (spots == place_ref[1:2, :])
        chosen = jnp.where(chosen, 1.0, 0.0).astype(jnp.bfloat16)
        total = total + lax.dot_general(
            patch_ref[...], chosen, TN, preferred_element_type=jnp.float32
        )
        begin += count
    ordered = jnp.where(place_ref[2:3, :] == 0, total[:width], total[width:]).astype(jnp.bfloat16)
    embedded = lax.dot_general(ordered, embed_ref[...], TN, preferred_element_type=jnp.float32)
    center = jnp.mean(embedded, axis=-1, keepdims=True)
    centered = embedded - center
    variance = jnp.mean(centered * centered, axis=-1, keepdims=True)
    normed = centered * lax.rsqrt(variance + 1e-06)
    out_ref[...] = (normed * (1.0 + scale_ref[...]) + shift_ref[...]).astype(out_ref.dtype)


def along_line(unit):
    return [unit] + [xor_permute(unit, "ctx", 4 * step) for step in (1, 2, 3)]


def round_square(line):
    return xor_permute(line, "ctx", 2), xor_permute(line, "groups", 1)


def to_corner(across, other):
    return xor_permute(other[:2], "ctx", 2), xor_permute(across[2:], "groups", 1)


def both_cores(pieces):
    return list(pieces) + [xor_permute(piece, "ctx", 1) for piece in pieces]


def unit_channel_map(grid, group, device, unit_channels, units):
    unit = jnp.arange(units * SUBLANES, dtype=jnp.int32) // SUBLANES
    within = jnp.arange(units * SUBLANES, dtype=jnp.int32) % SUBLANES
    if grid:
        step, kind, core = unit % 4, unit // 4 % 4, unit // 16
        source = device ^ (4 * step + 2 * (kind % 2) + core)
        unit = source * 2 + (group ^ (kind // 2))
    return jnp.where(within < unit_channels, unit * unit_channels + within, -1)


def body(
    features,
    clip_ids,
    gain_first,
    weight_first,
    gain_second,
    weight_second,
    gain_third,
    weight_out,
    embed_weight,
    shift_mod,
    scale_mod,
    token_order,
):
    frames, height, breadth, channels = features.shape
    taps = weight_first.shape[0]
    groups, devices = lax.axis_size("groups"), lax.axis_size("ctx")
    group, device = lax.axis_index("groups"), lax.axis_index("ctx")
    grid = groups == 2 and devices == 16
    units = 32
    unit_channels = channels // units

    by_output = [weight.transpose(2, 0, 1) for weight in (weight_first, weight_second)]
    channel_map = unit_channel_map(grid, group, device, unit_channels, units)
    pick = (channel_map[:, None] == jnp.arange(channels, dtype=jnp.int32)).astype(jnp.bfloat16)
    wide = expand_weight_out(weight_out.transpose(0, 2, 1))
    turned = features.transpose(0, 2, 1, 3)
    turned_rim = to_next(features[frames - 2 :], "ctx").transpose(0, 2, 1, 3)

    spots = (height // 2) * (breadth // 2)
    frame, spot = token_order // spots, token_order % spots
    spot = spot % (breadth // 2) * (height // 2) + spot // (breadth // 2)
    owner = frame // frames

    def piece_of(source):
        if not grid:
            return source
        away = source ^ device
        return (away % 2 * 2 + away // 2 % 2) * 4 + away // 4

    own_place = piece_of(owner) * 2 * spots + spot
    sent_place = jnp.where(owner > 0, (piece_of(jnp.maximum(owner - 1, 0)) * 2 + 1) * spots + spot, -1)
    place = jnp.stack([own_place, sent_place, frame % frames])

    if grid:
        half = group.astype(jnp.int32).reshape(1)
        packed_first, packed_second = pack_units(half, by_output, unit_channels)
        line_first = along_line(packed_first)
        line_first, wide, pick, place, turned, turned_rim = lax.optimization_barrier(
            (line_first, wide, pick, place, turned, turned_rim)
        )
        line_first = jnp.stack(line_first)
        packed_second, line_first = lax.optimization_barrier((packed_second, line_first))
        square_first = round_square(line_first)
        line_second = along_line(packed_second)
        line_first, square_first, line_second = lax.optimization_barrier(
            (line_first, square_first, line_second)
        )
        corner_first = to_corner(*square_first)
        line_second, corner_first = lax.optimization_barrier((line_second, corner_first))
        line_second = jnp.stack(line_second)
        square_second = round_square(line_second)
        units_first = both_cores((line_first, *square_first, *corner_first))
    else:
        units_first, units_second = [
            [pack_whole(lax.all_gather(weight, "ctx", axis=0, tiled=True), units)]
            for weight in by_output
        ]

    first = (device * frames).astype(jnp.int32).reshape(1)
    scratch = conv_scratch(frames, breadth, height, taps, units * SUBLANES)
    image = pltpu.VMEM((frames, breadth, height, channels), jnp.bfloat16)
    second_in = pl.pallas_call(
        functools.partial(first_kernel, taps=taps, unit_channels=unit_channels),
        out_shape=image,
        in_specs=[SMEM_SPEC] * 2 + [VMEM_SPEC] * (5 + len(units_first)),
        out_specs=VMEM_SPEC,
        scratch_shapes=scratch,
        compiler_params=LARGE,
    )(
        clip_ids, first, IN_VMEM(turned), IN_VMEM(turned_rim), gain_first.reshape(1, -1),
        gain_second.reshape(1, -1), IN_VMEM(pick), *map(IN_VMEM, units_first),
    )
    second_rim = to_next(second_in[frames - 2 :], "ctx")
    if grid:
        line_second, square_second, second_in = lax.optimization_barrier(
            (line_second, square_second, second_in)
        )
        corner_second = to_corner(*square_second)
        units_second = both_cores((line_second, *square_second, *corner_second))

    depth = weight_out.shape[2]
    parts = pl.pallas_call(
        functools.partial(second_kernel, taps=taps, unit_channels=unit_channels),
        out_shape=pltpu.VMEM((2 * spots, frames * 4 * depth), jnp.bfloat16),
        in_specs=[SMEM_SPEC] * 2 + [VMEM_SPEC] * (6 + len(units_second)),
        out_specs=VMEM_SPEC,
        scratch_shapes=scratch
        + [
            pltpu.VMEM((2, frames * breadth * height, LANES), jnp.float32),
            pltpu.VMEM((4, 2, frames, breadth + 2, height // 2, LANES), jnp.float32),
        ],
        compiler_params=LARGE,
    )(
        clip_ids, first, IN_VMEM(second_in), IN_VMEM(second_rim), IN_VMEM(turned),
        gain_third.reshape(1, -1), IN_VMEM(pick), IN_VMEM(wide), *map(IN_VMEM, units_second),
    )
    if grid:
        line = jnp.concatenate(along_line(parts))
        pieces = both_cores((line, xor_permute(line, "ctx", 2)))
    else:
        pieces = [lax.all_gather(parts, "ctx", axis=0, tiled=True)]

    tokens, width = token_order.shape[0], embed_weight.shape[1]
    return pl.pallas_call(
        embed_kernel,
        out_shape=jax.ShapeDtypeStruct((tokens, width), jnp.bfloat16),
        in_specs=[VMEM_SPEC] * (4 + len(pieces)),
        out_specs=VMEM_SPEC,
        compiler_params=LARGE,
    )(
        IN_VMEM(place), IN_VMEM(embed_weight), scale_mod.reshape(1, -1), shift_mod.reshape(1, -1),
        *map(IN_VMEM, pieces),
    )


def solution(mesh):
    in_specs = (
        P(("groups", "ctx"), None, None, None),
        P("groups"),
        P(),
        P(None, None, "ctx"),
        P(),
        P(None, None, "ctx"),
        P(),
        P(),
        P(),
        P(),
        P(),
        P(("groups", "ctx")),
    )
    out_specs = P(("groups", "ctx"), None)
    return jax.shard_map(body, mesh=mesh, in_specs=in_specs, out_specs=out_specs, check_vma=False)
```

```python
import functools

import jax
import jax.numpy as jnp
from jax import lax
from jax.experimental import pallas as pl
from jax.experimental.pallas import tpu as pltpu
from jax.sharding import PartitionSpec as P

LANES = 128
SUBLANES = 8
UNIT_ROWS = 256
SCRATCH_ROWS = 288
NT = (((1,), (1,)), ((), ()))
TN = (((0,), (0,)), ((), ()))
VMEM_SPEC = pl.BlockSpec(memory_space=pltpu.VMEM)
SMEM_SPEC = pl.BlockSpec(memory_space=pltpu.SMEM)
IN_VMEM = functools.partial(pltpu.with_memory_space_constraint, memory_space=pltpu.VMEM)
IN_HBM = functools.partial(pltpu.with_memory_space_constraint, memory_space=pltpu.HBM)
SMALL = pltpu.CompilerParams(vmem_limit_bytes=4 * 2**20)
LARGE = pltpu.CompilerParams(vmem_limit_bytes=24 * 2**20)


def xor_permute(value, axis, mask):
    count = lax.axis_size(axis)
    return lax.ppermute(value, axis, [(source, source ^ mask) for source in range(count)])


def to_next(value, axis):
    count = lax.axis_size(axis)
    return lax.ppermute(value, axis, [(source, source + 1) for source in range(count - 1)])


def unit_geometry(taps, unit_channels):
    pairs = (taps + 1) // 2
    head_rows = -(-unit_channels * taps // SUBLANES) * SUBLANES
    return pairs, head_rows


def pack_kernel(half_ref, *refs, unit_channels):
    *weight_refs, unit_ref, staged = refs
    for index, weight_ref in enumerate(weight_refs):
        _, taps, channels = weight_ref.shape
        pairs, head_rows = unit_geometry(taps, unit_channels)
        tail = channels - LANES
        staged[...] = jnp.zeros_like(staged)
        for channel in range(unit_channels):
            rows = weight_ref[half_ref[0] * unit_channels + channel].astype(jnp.float32)
            staged[channel * taps : channel * taps + taps, :] = rows[:, :LANES]
            at = head_rows + channel * pairs
            staged[at : at + pairs, 0:tail] = rows[:pairs, LANES:]
            staged[at : at + taps - pairs, tail : 2 * tail] = rows[pairs:, LANES:]
        unit_ref[index] = staged[...].astype(jnp.bfloat16)


def pack_units(half, weights, unit_channels):
    return pl.pallas_call(
        functools.partial(pack_kernel, unit_channels=unit_channels),
        out_shape=pltpu.VMEM((len(weights), UNIT_ROWS, LANES), jnp.bfloat16),
        in_specs=[SMEM_SPEC] + [VMEM_SPEC] * len(weights),
        out_specs=VMEM_SPEC,
        scratch_shapes=[pltpu.VMEM((UNIT_ROWS, LANES), jnp.float32)],
        compiler_params=SMALL,
    )(half, *map(IN_HBM, weights))


def pack_whole(weight, units):
    outputs, taps, channels = weight.shape
    unit_channels = outputs // units
    pairs, head_rows = unit_geometry(taps, unit_channels)
    split = weight.reshape(units, unit_channels, taps, channels)
    head = split[..., :LANES].reshape(units, unit_channels * taps, LANES)
    head = jnp.pad(head, ((0, 0), (0, head_rows - unit_channels * taps), (0, 0)))
    low, high = split[:, :, :pairs, LANES:], split[:, :, pairs:, LANES:]
    high = jnp.pad(high, ((0, 0), (0, 0), (0, 2 * pairs - taps), (0, 0)))
    tail = jnp.concatenate([low, high], axis=-1).reshape(units, unit_channels * pairs, LANES)
    both = jnp.concatenate([head, tail], axis=1)
    return jnp.pad(both, ((0, 0), (0, UNIT_ROWS - both.shape[1]), (0, 0)))


def expand_kernel(weight_ref, wide_ref):
    depth, channels = weight_ref.shape[1:]
    wide_ref[...] = jnp.zeros_like(wide_ref)
    for u in range(4):
        for v in range(4):
            for a in range(3):
                for r in range(2):
                    for s in range(2):
                        if 0 <= u - r <= 2 and 0 <= v - s <= 2:
                            at = ((a * 2 + r) * 2 + s) * depth
                            wide_ref[4 * u + v, at : at + depth, :channels] = weight_ref[
                                9 * a + 3 * (u - r) + (v - s)
                            ]


def expand_weight_out(weight):
    _, depth, channels = weight.shape
    return pl.pallas_call(
        expand_kernel,
        out_shape=pltpu.VMEM((16, 12 * depth, 2 * LANES), jnp.bfloat16),
        in_specs=[VMEM_SPEC],
        out_specs=VMEM_SPEC,
        compiler_params=SMALL,
    )(IN_HBM(weight))


def rms_silu(values, gain_vector):
    normed = (
        values * lax.rsqrt(jnp.mean(values * values, axis=-1, keepdims=True) + 1e-06) * gain_vector
    )
    return jax.nn.silu(normed)


def same_clip(clips_ref, frame, steps_back):
    earlier = jnp.maximum(frame - steps_back, 0)
    return (frame >= steps_back) & (clips_ref[earlier] == clips_ref[frame])


def split_lanes(values):
    tail = values[:, LANES:]
    fill = jnp.zeros((values.shape[0], 2 * LANES - values.shape[1]), values.dtype)
    return values[:, :LANES], jnp.concatenate([tail, fill], axis=1)


def place_frame(values, at, head_x, low_x, high_x):
    breadth, height = head_x.shape[2] - 2, head_x.shape[3]
    row = lax.broadcasted_iota(jnp.int32, (values.shape[0], LANES), 0) % height
    head, tail = split_lanes(values)
    count = values.shape[0]
    for tap in range(3):
        for part, part_x in ((head, head_x), (tail, low_x)):
            if tap == 0:
                part = jnp.where(row == 0, 0.0, pltpu.roll(part, 1, 0))
            if tap == 2:
                part = jnp.where(row == height - 1, 0.0, pltpu.roll(part, count - 1, 0))
            part_x[tap, at, 1 : breadth + 1] = part.reshape(breadth, height, LANES).astype(
                jnp.bfloat16
            )
            if part_x is low_x:
                high_x[tap, at, 1 : breadth + 1] = (
                    pltpu.roll(part, LANES // 2, 1).reshape(breadth, height, LANES)
                ).astype(jnp.bfloat16)


def clear_rims(arrays):
    for array in arrays:
        frames, wide = array.shape[1], array.shape[2]
        array[:, frames - 1] = jnp.zeros_like(array[:, frames - 1])
        array[:, :, 0] = jnp.zeros_like(array[:, :, 0])
        array[:, :, wide - 1] = jnp.zeros_like(array[:, :, wide - 1])


def unpack_units(unit_refs, rhs, staged, taps, unit_channels):
    pairs, head_rows = unit_geometry(taps, unit_channels)
    staged[:, UNIT_ROWS:] = jnp.zeros_like(staged[:, UNIT_ROWS:])
    done = 0
    for unit_ref in unit_refs:
        couples = unit_ref.shape[0] // 2

        def couple_step(couple, carry, unit_ref=unit_ref, done=done):
            for one in range(2):
                staged[one, :UNIT_ROWS] = unit_ref[2 * couple + one].astype(jnp.float32)
            to = pl.ds(pl.multiple_of((done + couple) * 16, 16), 16)
            for tap in range(taps):
                rows = [staged[one, pl.ds(tap, 8, stride=taps), :] for one in range(2)]
                rhs[tap, to, :] = jnp.concatenate(rows, axis=0).astype(jnp.bfloat16)
            for pair in range(pairs):
                rows = [staged[one, pl.ds(head_rows + pair, 8, stride=pairs), :] for one in range(2)]
                rhs[taps + pair, to, :] = jnp.concatenate(rows, axis=0).astype(jnp.bfloat16)
            return carry

        lax.fori_loop(0, couples, couple_step, 0)
        done += couples


def convolve(clips_ref, first, head_x, low_x, high_x, rhs, frames, taps):
    zero_frame = head_x.shape[1] - 1
    breadth, height = head_x.shape[2] - 2, head_x.shape[3]
    pairs = (taps + 1) // 2
    source = [
        [
            jnp.where(same_clip(clips_ref, first + frame, 2 - tap), frame + tap, zero_frame)
            for tap in range(3)
        ]
        for frame in range(frames)
    ]

    def shifted(array, tap):
        a, b, e = tap // 9, tap // 3 % 3, tap % 3
        return jnp.concatenate(
            [
                array[b, source[frame][a], e : e + breadth].reshape(breadth * height, LANES)
                for frame in range(frames)
            ],
            axis=0,
        )

    def chunk(index):
        if index < taps:
            return shifted(head_x, index)
        pair = index - taps
        low = shifted(low_x, pair)
        return low + shifted(high_x, pair + pairs) if pair + pairs < taps else low

    total = taps + pairs
    summed = None
    for begin in range(0, total, 14):
        end = min(begin + 14, total)
        part = lax.dot_general(
            jnp.concatenate([chunk(index) for index in range(begin, end)], axis=1),
            jnp.concatenate([rhs[index] for index in range(begin, end)], axis=1),
            NT,
            preferred_element_type=jnp.float32,
        )
        summed = part if summed is None else summed + part
    return summed


def first_kernel(
    clips_ref, first_ref, own_ref, rim_ref, gain_first_ref, gain_second_ref, pick_ref, *rest,
    taps, unit_channels,
):
    *unit_refs, out_ref, head_x, low_x, high_x, rhs, staged = rest
    frames, breadth, height, channels = own_ref.shape
    clear_rims((head_x, low_x, high_x))
    for frame in range(frames + 2):
        values = rim_ref[frame] if frame < 2 else own_ref[frame - 2]
        values = values.astype(jnp.float32).reshape(breadth * height, channels)
        place_frame(rms_silu(values, gain_first_ref[...]), frame, head_x, low_x, high_x)
    unpack_units(unit_refs, rhs, staged, taps, unit_channels)
    summed = convolve(clips_ref, first_ref[0], head_x, low_x, high_x, rhs, frames, taps)
    first_out = jnp.dot(
        summed.astype(jnp.bfloat16), pick_ref[...], preferred_element_type=jnp.float32
    )
    out_ref[...] = (
        rms_silu(first_out, gain_second_ref[...])
        .astype(jnp.bfloat16)
        .reshape(frames, breadth, height, channels)
    )


def second_kernel(
    clips_ref, first_ref, own_ref, rim_ref, features_ref, gain_ref, pick_ref, wide_ref, *rest,
    taps, unit_channels,
):
    *unit_refs, parts_out, head_x, low_x, high_x, rhs, staged, plain, windows = rest
    frames, breadth, height, channels = own_ref.shape
    pixels = breadth * height
    rows, columns = height // 2, breadth // 2
    width = wide_ref.shape[1] // 3
    first = first_ref[0]
    clear_rims((head_x, low_x, high_x))
    for frame in range(frames + 2):
        values = rim_ref[frame] if frame < 2 else own_ref[frame - 2]
        values = values.astype(jnp.float32).reshape(pixels, channels)
        place_frame(values, frame, head_x, low_x, high_x)
    unpack_units(unit_refs, rhs, staged, taps, unit_channels)
    summed = convolve(clips_ref, first, head_x, low_x, high_x, rhs, frames, taps)
    features = lax.dot_general(
        features_ref[...].reshape(frames * pixels, channels),
        pick_ref[...],
        NT,
        preferred_element_type=jnp.float32,
    )
    block_out = jnp.dot(
        (features + summed).astype(jnp.bfloat16), pick_ref[...], preferred_element_type=jnp.float32
    )
    head_in = rms_silu(block_out, gain_ref[...])
    for part, values in enumerate(split_lanes(head_in)):
        plain[part] = values
    windows[...] = jnp.zeros_like(windows)
    half = frames * pixels // 2
    row = lax.broadcasted_iota(jnp.int32, (half, LANES), 0) % rows
    for part in range(2):
        even = plain[part, pl.ds(0, half, stride=2), :]
        odd = plain[part, pl.ds(1, half, stride=2), :]
        before = jnp.where(row == 0, 0.0, pltpu.roll(odd, 1, 0))
        after = jnp.where(row == rows - 1, 0.0, pltpu.roll(even, half - 1, 0))
        for u, values in enumerate((before, even, odd, after)):
            windows[u, part, :, 1 : breadth + 1] = values.reshape(frames, breadth, rows, LANES)
    chunks = []
    for u in range(4):
        for v in range(4):
            for part in range(2):
                chunks.append(
                    jnp.concatenate(
                        [
                            windows[u, part, frame, pl.ds(v, columns, stride=2)].reshape(
                                columns * rows, LANES
                            )
                            for frame in range(frames)
                        ],
                        axis=0,
                    ).astype(jnp.bfloat16)
                )
    outs = lax.dot_general(
        jnp.concatenate(chunks, axis=1),
        jnp.concatenate([wide_ref[window] for window in range(16)], axis=1),
        NT,
        preferred_element_type=jnp.float32,
    )
    spots = columns * rows

    def from_frame(frame, tap):
        return outs[frame * spots : (frame + 1) * spots, tap * width : (tap + 1) * width]

    def gathered(frame, sources):
        total = jnp.zeros((spots, width), jnp.float32)
        for tap in range(3):
            source = frame + tap - 2
            if source in sources:
                kept = same_clip(clips_ref, jnp.minimum(first + frame, clips_ref.shape[0] - 1), 2 - tap)
                total = total + jnp.where(kept, from_frame(source, tap), 0.0)
        return total

    own = range(frames)
    parts = [
        jnp.concatenate([gathered(frame + ahead, own) for frame in own], axis=1)
        for ahead in (0, frames)
    ]
    parts_out[...] = jnp.concatenate(parts, axis=0).astype(jnp.bfloat16)


def conv_scratch(frames, breadth, height, taps, outputs):
    pairs = (taps + 1) // 2
    image = pltpu.VMEM((3, frames + 3, breadth + 2, height, LANES), jnp.bfloat16)
    return [image] * 3 + [
        pltpu.VMEM((taps + pairs, outputs, LANES), jnp.bfloat16),
        pltpu.VMEM((2, SCRATCH_ROWS, LANES), jnp.float32),
    ]


def embed_kernel(place_ref, embed_ref, scale_ref, shift_ref, *rest):
    *patch_refs, out_ref = rest
    width = embed_ref.shape[0]
    tokens = out_ref.shape[0]
    total = jnp.zeros((LANES, tokens), jnp.float32)
    begin = 0
    for patch_ref in patch_refs:
        count = patch_ref.shape[0]
        spots = lax.broadcasted_iota(jnp.int32, (count, tokens), 0) + begin
        chosen = (spots == place_ref[0:1, :]) | (spots == place_ref[1:2, :])
        chosen = jnp.where(chosen, 1.0, 0.0).astype(jnp.bfloat16)
        total = total + lax.dot_general(
            patch_ref[...], chosen, TN, preferred_element_type=jnp.float32
        )
        begin += count
    ordered = jnp.where(place_ref[2:3, :] == 0, total[:width], total[width:]).astype(jnp.bfloat16)
    embedded = lax.dot_general(ordered, embed_ref[...], TN, preferred_element_type=jnp.float32)
    center = jnp.mean(embedded, axis=-1, keepdims=True)
    centered = embedded - center
    variance = jnp.mean(centered * centered, axis=-1, keepdims=True)
    normed = centered * lax.rsqrt(variance + 1e-06)
    out_ref[...] = (normed * (1.0 + scale_ref[...]) + shift_ref[...]).astype(out_ref.dtype)


def along_line(unit):
    return [unit] + [xor_permute(unit, "ctx", 4 * step) for step in (1, 2, 3)]


def round_square(half_line):
    return xor_permute(half_line, "ctx", 2), xor_permute(half_line, "groups", 1)


def in_unit_order(low, high, across, other, corners):
    return [low, high, *across, *other, *corners]


def both_cores(pieces):
    return list(pieces) + [xor_permute(piece, "ctx", 1) for piece in pieces]


def unit_channel_map(grid, group, device, unit_channels, units):
    unit = jnp.arange(units * SUBLANES, dtype=jnp.int32) // SUBLANES
    within = jnp.arange(units * SUBLANES, dtype=jnp.int32) % SUBLANES
    if grid:
        step, kind, core = unit % 4, unit // 4 % 4, unit // 16
        source = device ^ (4 * step + 2 * (kind % 2) + core)
        unit = source * 2 + (group ^ (kind // 2))
    return jnp.where(within < unit_channels, unit * unit_channels + within, -1)


def body(
    features,
    clip_ids,
    gain_first,
    weight_first,
    gain_second,
    weight_second,
    gain_third,
    weight_out,
    embed_weight,
    shift_mod,
    scale_mod,
    token_order,
):
    frames, height, breadth, channels = features.shape
    taps = weight_first.shape[0]
    groups, devices = lax.axis_size("groups"), lax.axis_size("ctx")
    group, device = lax.axis_index("groups"), lax.axis_index("ctx")
    grid = groups == 2 and devices == 16
    units = 32
    unit_channels = channels // units

    by_output = [weight.transpose(2, 0, 1) for weight in (weight_first, weight_second)]
    channel_map = unit_channel_map(grid, group, device, unit_channels, units)
    pick = (channel_map[:, None] == jnp.arange(channels, dtype=jnp.int32)).astype(jnp.bfloat16)
    wide = expand_weight_out(weight_out.transpose(0, 2, 1))
    turned = features.transpose(0, 2, 1, 3)
    turned_rim = to_next(features[frames - 2 :], "ctx").transpose(0, 2, 1, 3)

    spots = (height // 2) * (breadth // 2)
    frame, spot = token_order // spots, token_order % spots
    spot = spot % (breadth // 2) * (height // 2) + spot // (breadth // 2)
    owner = frame // frames

    def piece_of(source):
        if not grid:
            return source
        away = source ^ device
        return (away % 2 * 2 + away // 2 % 2) * 4 + away // 4

    own_place = piece_of(owner) * 2 * spots + spot
    sent_place = jnp.where(owner > 0, (piece_of(jnp.maximum(owner - 1, 0)) * 2 + 1) * spots + spot, -1)
    place = jnp.stack([own_place, sent_place, frame % frames])

    if grid:
        half = group.astype(jnp.int32).reshape(1)
        line = along_line(pack_units(half, by_output, unit_channels))
        lows = [jnp.stack([part[index] for part in line[:2]]) for index in range(2)]
        low_squares = round_square(lows[0])
        line, wide, pick, place, turned = lax.optimization_barrier(
            (line, wide, pick, place, turned)
        )
        highs = [jnp.stack([part[index] for part in line[2:]]) for index in range(2)]
        high_squares = round_square(highs[0])
        across, other = zip(low_squares, high_squares)
        corners = xor_permute(other[0], "ctx", 2), xor_permute(across[1], "groups", 1)
        lows, highs, corners, turned_rim = lax.optimization_barrier(
            (lows, highs, corners, turned_rim)
        )
        units_first = both_cores(in_unit_order(lows[0], highs[0], across, other, corners))
        across, other = zip(round_square(lows[1]), round_square(highs[1]))
        corners = xor_permute(other[0], "ctx", 2), xor_permute(across[1], "groups", 1)
        units_second = in_unit_order(lows[1], highs[1], across, other, corners)
    else:
        units_first, units_second = [
            [pack_whole(lax.all_gather(weight, "ctx", axis=0, tiled=True), units)]
            for weight in by_output
        ]

    first = (device * frames).astype(jnp.int32).reshape(1)
    scratch = conv_scratch(frames, breadth, height, taps, units * SUBLANES)
    image = pltpu.VMEM((frames, breadth, height, channels), jnp.bfloat16)
    second_in = pl.pallas_call(
        functools.partial(first_kernel, taps=taps, unit_channels=unit_channels),
        out_shape=image,
        in_specs=[SMEM_SPEC] * 2 + [VMEM_SPEC] * (5 + len(units_first)),
        out_specs=VMEM_SPEC,
        scratch_shapes=scratch,
        compiler_params=LARGE,
    )(
        clip_ids, first, IN_VMEM(turned), IN_HBM(turned_rim), gain_first.reshape(1, -1),
        gain_second.reshape(1, -1), IN_VMEM(pick), *map(IN_HBM, units_first),
    )
    second_rim = to_next(second_in[frames - 2 :], "ctx")
    if grid:
        units_second, second_in = lax.optimization_barrier((units_second, second_in))
        units_second = both_cores(units_second)

    depth = weight_out.shape[2]
    parts = pl.pallas_call(
        functools.partial(second_kernel, taps=taps, unit_channels=unit_channels),
        out_shape=pltpu.VMEM((2 * spots, frames * 4 * depth), jnp.bfloat16),
        in_specs=[SMEM_SPEC] * 2 + [VMEM_SPEC] * (6 + len(units_second)),
        out_specs=VMEM_SPEC,
        scratch_shapes=scratch
        + [
            pltpu.VMEM((2, frames * breadth * height, LANES), jnp.float32),
            pltpu.VMEM((4, 2, frames, breadth + 2, height // 2, LANES), jnp.float32),
        ],
        compiler_params=LARGE,
    )(
        clip_ids, first, IN_VMEM(second_in), IN_VMEM(second_rim), IN_VMEM(turned),
        gain_third.reshape(1, -1), IN_VMEM(pick), IN_VMEM(wide), *map(IN_HBM, units_second),
    )
    if grid:
        line = jnp.concatenate(along_line(parts))
        pieces = both_cores((line, xor_permute(line, "ctx", 2)))
    else:
        pieces = [lax.all_gather(parts, "ctx", axis=0, tiled=True)]

    tokens, width = token_order.shape[0], embed_weight.shape[1]
    return pl.pallas_call(
        embed_kernel,
        out_shape=jax.ShapeDtypeStruct((tokens, width), jnp.bfloat16),
        in_specs=[VMEM_SPEC] * (4 + len(pieces)),
        out_specs=VMEM_SPEC,
        compiler_params=LARGE,
    )(
        IN_VMEM(place), IN_VMEM(embed_weight), scale_mod.reshape(1, -1), shift_mod.reshape(1, -1),
        *map(IN_VMEM, pieces),
    )


def solution(mesh):
    in_specs = (
        P(("groups", "ctx"), None, None, None),
        P("groups"),
        P(),
        P(None, None, "ctx"),
        P(),
        P(None, None, "ctx"),
        P(),
        P(),
        P(),
        P(),
        P(),
        P(("groups", "ctx")),
    )
    out_specs = P(("groups", "ctx"), None)
    return jax.shard_map(body, mesh=mesh, in_specs=in_specs, out_specs=out_specs, check_vma=False)
```

```python
import functools

import jax
import jax.numpy as jnp
from jax import lax
from jax.experimental import pallas as pl
from jax.experimental.pallas import tpu as pltpu
from jax.sharding import PartitionSpec as P

LANES = 128
SUBLANES = 8
UNIT_ROWS = 256
SCRATCH_ROWS = 288
NT = (((1,), (1,)), ((), ()))
TN = (((0,), (0,)), ((), ()))
VMEM_SPEC = pl.BlockSpec(memory_space=pltpu.VMEM)
SMEM_SPEC = pl.BlockSpec(memory_space=pltpu.SMEM)
IN_VMEM = functools.partial(pltpu.with_memory_space_constraint, memory_space=pltpu.VMEM)
IN_HBM = functools.partial(pltpu.with_memory_space_constraint, memory_space=pltpu.HBM)
SMALL = pltpu.CompilerParams(vmem_limit_bytes=4 * 2**20)
LARGE = pltpu.CompilerParams(vmem_limit_bytes=24 * 2**20)


def xor_permute(value, axis, mask):
    count = lax.axis_size(axis)
    return lax.ppermute(value, axis, [(source, source ^ mask) for source in range(count)])


def to_next(value, axis):
    count = lax.axis_size(axis)
    return lax.ppermute(value, axis, [(source, source + 1) for source in range(count - 1)])


def unit_geometry(taps, unit_channels):
    pairs = (taps + 1) // 2
    head_rows = -(-unit_channels * taps // SUBLANES) * SUBLANES
    return pairs, head_rows


def pack_kernel(half_ref, *refs, unit_channels):
    *weight_refs, unit_ref, staged = refs
    for index, weight_ref in enumerate(weight_refs):
        _, taps, channels = weight_ref.shape
        pairs, head_rows = unit_geometry(taps, unit_channels)
        tail = channels - LANES
        staged[...] = jnp.zeros_like(staged)
        for channel in range(unit_channels):
            rows = weight_ref[half_ref[0] * unit_channels + channel].astype(jnp.float32)
            staged[channel * taps : channel * taps + taps, :] = rows[:, :LANES]
            at = head_rows + channel * pairs
            staged[at : at + pairs, 0:tail] = rows[:pairs, LANES:]
            staged[at : at + taps - pairs, tail : 2 * tail] = rows[pairs:, LANES:]
        unit_ref[index] = staged[...].astype(jnp.bfloat16)


def pack_units(half, weights, unit_channels):
    return pl.pallas_call(
        functools.partial(pack_kernel, unit_channels=unit_channels),
        out_shape=pltpu.VMEM((len(weights), UNIT_ROWS, LANES), jnp.bfloat16),
        in_specs=[SMEM_SPEC] + [VMEM_SPEC] * len(weights),
        out_specs=VMEM_SPEC,
        scratch_shapes=[pltpu.VMEM((UNIT_ROWS, LANES), jnp.float32)],
        compiler_params=SMALL,
    )(half, *map(IN_HBM, weights))


def pack_whole(weight, units):
    outputs, taps, channels = weight.shape
    unit_channels = outputs // units
    pairs, head_rows = unit_geometry(taps, unit_channels)
    split = weight.reshape(units, unit_channels, taps, channels)
    head = split[..., :LANES].reshape(units, unit_channels * taps, LANES)
    head = jnp.pad(head, ((0, 0), (0, head_rows - unit_channels * taps), (0, 0)))
    low, high = split[:, :, :pairs, LANES:], split[:, :, pairs:, LANES:]
    high = jnp.pad(high, ((0, 0), (0, 0), (0, 2 * pairs - taps), (0, 0)))
    tail = jnp.concatenate([low, high], axis=-1).reshape(units, unit_channels * pairs, LANES)
    both = jnp.concatenate([head, tail], axis=1)
    return jnp.pad(both, ((0, 0), (0, UNIT_ROWS - both.shape[1]), (0, 0)))


def expand_kernel(weight_ref, wide_ref):
    depth, channels = weight_ref.shape[1:]
    wide_ref[...] = jnp.zeros_like(wide_ref)
    for u in range(4):
        for v in range(4):
            for a in range(3):
                for r in range(2):
                    for s in range(2):
                        if 0 <= u - r <= 2 and 0 <= v - s <= 2:
                            at = ((a * 2 + r) * 2 + s) * depth
                            wide_ref[4 * u + v, at : at + depth, :channels] = weight_ref[
                                9 * a + 3 * (u - r) + (v - s)
                            ]


def expand_weight_out(weight):
    _, depth, channels = weight.shape
    return pl.pallas_call(
        expand_kernel,
        out_shape=pltpu.VMEM((16, 12 * depth, 2 * LANES), jnp.bfloat16),
        in_specs=[VMEM_SPEC],
        out_specs=VMEM_SPEC,
        compiler_params=SMALL,
    )(IN_HBM(weight))


def rms_silu(values, gain_vector):
    normed = (
        values * lax.rsqrt(jnp.mean(values * values, axis=-1, keepdims=True) + 1e-06) * gain_vector
    )
    return jax.nn.silu(normed)


def same_clip(clips_ref, frame, steps_back):
    earlier = jnp.maximum(frame - steps_back, 0)
    return (frame >= steps_back) & (clips_ref[earlier] == clips_ref[frame])


def split_lanes(values):
    tail = values[:, LANES:]
    fill = jnp.zeros((values.shape[0], 2 * LANES - values.shape[1]), values.dtype)
    return values[:, :LANES], jnp.concatenate([tail, fill], axis=1)


def place_frame(head, tail, at, head_x, low_x, high_x):
    breadth, height = head_x.shape[2] - 2, head_x.shape[3]
    row = lax.broadcasted_iota(jnp.int32, head.shape, 0) % height
    count = head.shape[0]
    for tap in range(3):
        for part, part_x in ((head, head_x), (tail, low_x)):
            if tap == 0:
                part = jnp.where(row == 0, 0.0, pltpu.roll(part, 1, 0))
            if tap == 2:
                part = jnp.where(row == height - 1, 0.0, pltpu.roll(part, count - 1, 0))
            part_x[tap, at, 1 : breadth + 1] = part.reshape(breadth, height, LANES).astype(
                jnp.bfloat16
            )
            if part_x is low_x:
                high_x[tap, at, 1 : breadth + 1] = (
                    pltpu.roll(part, LANES // 2, 1).reshape(breadth, height, LANES)
                ).astype(jnp.bfloat16)


def clear_rims(arrays):
    for array in arrays:
        frames, wide = array.shape[1], array.shape[2]
        array[:, frames - 1] = jnp.zeros_like(array[:, frames - 1])
        array[:, :, 0] = jnp.zeros_like(array[:, :, 0])
        array[:, :, wide - 1] = jnp.zeros_like(array[:, :, wide - 1])


def unpack_kernel(*refs, taps, unit_channels):
    *unit_refs, rhs, staged = refs
    pairs, head_rows = unit_geometry(taps, unit_channels)
    staged[:, UNIT_ROWS:] = jnp.zeros_like(staged[:, UNIT_ROWS:])
    done = 0
    for unit_ref in unit_refs:
        couples = unit_ref.shape[0] // 2

        def couple_step(couple, carry, unit_ref=unit_ref, done=done):
            for one in range(2):
                staged[one, :UNIT_ROWS] = unit_ref[2 * couple + one].astype(jnp.float32)
            to = pl.ds(pl.multiple_of((done + couple) * 16, 16), 16)
            for tap in range(taps):
                rows = [staged[one, pl.ds(tap, 8, stride=taps), :] for one in range(2)]
                rhs[tap, to, :] = jnp.concatenate(rows, axis=0).astype(jnp.bfloat16)
            for pair in range(pairs):
                rows = [staged[one, pl.ds(head_rows + pair, 8, stride=pairs), :] for one in range(2)]
                rhs[taps + pair, to, :] = jnp.concatenate(rows, axis=0).astype(jnp.bfloat16)
            return carry

        lax.fori_loop(0, couples, couple_step, 0)
        done += couples


def unpack_units(pieces, taps, unit_channels, keep=IN_HBM):
    count = sum(piece.shape[0] for piece in pieces)
    return pl.pallas_call(
        functools.partial(unpack_kernel, taps=taps, unit_channels=unit_channels),
        out_shape=pltpu.VMEM((taps + (taps + 1) // 2, count * SUBLANES, LANES), jnp.bfloat16),
        in_specs=[VMEM_SPEC] * len(pieces),
        out_specs=VMEM_SPEC,
        scratch_shapes=[pltpu.VMEM((2, SCRATCH_ROWS, LANES), jnp.float32)],
        compiler_params=SMALL,
    )(*map(keep, pieces))


def convolve(clips_ref, first, frame, held, head_x, low_x, high_x, rhs_refs, taps):
    empty = head_x.shape[1] - 1
    breadth, height = head_x.shape[2] - 2, head_x.shape[3]
    pairs = (taps + 1) // 2
    sources = [
        jnp.where(same_clip(clips_ref, first + frame, 2 - tap), frame + tap - held[0], empty)
        for tap in range(3)
    ]

    def here(tap):
        return tap < taps and frame + tap // 9 in held

    def shifted(array, tap):
        a, b, e = tap // 9, tap // 3 % 3, tap % 3
        return array[b, sources[a], e : e + breadth].reshape(breadth * height, LANES)

    chunks = [(shifted(head_x, tap), tap) for tap in range(taps) if here(tap)]
    for pair in range(pairs):
        parts = []
        if here(pair):
            parts.append(shifted(low_x, pair))
        if here(pair + pairs):
            parts.append(shifted(high_x, pair + pairs))
        if parts:
            chunks.append((sum(parts[1:], parts[0]), taps + pair))
    summed = None
    for begin in range(0, len(chunks), 14):
        group = chunks[begin : begin + 14]
        part = lax.dot_general(
            jnp.concatenate([values for values, _ in group], axis=1),
            jnp.concatenate(
                [jnp.concatenate([rhs[index] for _, index in group], axis=1) for rhs in rhs_refs],
                axis=0,
            ),
            NT,
            preferred_element_type=jnp.float32,
        )
        summed = part if summed is None else summed + part
    return summed


def first_kernel(
    clips_ref, first_ref, own_ref, rim_ref, gain_first_ref, gain_second_ref, pick_ref, *rest,
    taps, unit_channels,
):
    *unit_refs, out_ref, sent_ref, head_x, low_x, high_x, rhs, staged = rest
    frames, breadth, height, channels = own_ref.shape
    clear_rims((head_x, low_x, high_x))
    for frame in range(frames + 2):
        values = rim_ref[frame] if frame < 2 else own_ref[frame - 2]
        values = values.astype(jnp.float32).reshape(breadth * height, channels)
        values = split_lanes(rms_silu(values, gain_first_ref[...]))
        place_frame(*values, frame, head_x, low_x, high_x)
    unpack_kernel(*unit_refs, rhs, staged, taps=taps, unit_channels=unit_channels)
    held = range(frames + 2)
    summed = jnp.concatenate(
        [
            convolve(clips_ref, first_ref[0], frame, held, head_x, low_x, high_x, [rhs], taps)
            for frame in range(frames)
        ],
        axis=0,
    )
    first_out = jnp.dot(
        summed.astype(jnp.bfloat16), pick_ref[...], preferred_element_type=jnp.float32
    )
    second_in = rms_silu(first_out, gain_second_ref[...])
    out_ref[...] = second_in.astype(jnp.bfloat16).reshape(frames, breadth, height, channels)
    pixels = breadth * height
    last = [second_in[at * pixels : (at + 1) * pixels] for at in (frames - 2, frames - 1)]
    sent_ref[0] = last[0][:, :LANES].astype(jnp.bfloat16)
    sent_ref[1] = last[1][:, :LANES].astype(jnp.bfloat16)
    tails = jnp.concatenate([values[:, LANES:] for values in last], axis=1)
    sent_ref[2] = tails.astype(jnp.bfloat16)


def own_kernel(
    clips_ref, first_ref, own_ref, features_ref, pick_ref, *rest, taps
):
    *rhs, summed_ref, head_x, low_x, high_x = rest
    frames, breadth, height, channels = own_ref.shape
    pixels = breadth * height
    clear_rims((head_x, low_x, high_x))
    for frame in range(frames):
        values = own_ref[frame].astype(jnp.float32).reshape(pixels, channels)
        place_frame(*split_lanes(values), frame, head_x, low_x, high_x)
    held = range(2, frames + 2)
    for frame in range(frames):
        features = lax.dot_general(
            features_ref[frame].reshape(pixels, channels),
            pick_ref[...],
            NT,
            preferred_element_type=jnp.float32,
        )
        summed_ref[frame * pixels : (frame + 1) * pixels] = features + convolve(
            clips_ref, first_ref[0], frame, held, head_x, low_x, high_x, rhs, taps
        )


def second_kernel(
    clips_ref, first_ref, rim_ref, gain_ref, pick_ref, wide_ref, summed_ref, *rest, taps
):
    *rhs, parts_out, head_x, low_x, high_x, plain, windows = rest
    breadth, height = head_x.shape[2] - 2, head_x.shape[3]
    pixels = breadth * height
    frames = summed_ref.shape[0] // pixels
    rows, columns = height // 2, breadth // 2
    width = wide_ref.shape[1] // 3
    first = first_ref[0]
    clear_rims((head_x, low_x, high_x))
    for frame in range(2):
        tail = rim_ref[2].astype(jnp.float32)
        if frame == 1:
            tail = pltpu.roll(tail, LANES // 2, 1)
        lane = lax.broadcasted_iota(jnp.int32, tail.shape, 1)
        tail = jnp.where(lane < LANES // 2, tail, 0.0)
        place_frame(rim_ref[frame].astype(jnp.float32), tail, frame, head_x, low_x, high_x)
    sums = []
    for frame in range(frames):
        total = summed_ref[frame * pixels : (frame + 1) * pixels]
        if frame < 2:
            total = total + convolve(
                clips_ref, first, frame, range(2), head_x, low_x, high_x, rhs, taps
            )
        sums.append(total.astype(jnp.bfloat16))
    block_out = jnp.dot(
        jnp.concatenate(sums, axis=0), pick_ref[...], preferred_element_type=jnp.float32
    )
    head_in = rms_silu(block_out, gain_ref[...])
    for part, values in enumerate(split_lanes(head_in)):
        plain[part] = values
    for at in (0, breadth + 1):
        windows[:, :, :, at] = jnp.zeros_like(windows[:, :, :, at])
    half = frames * pixels // 2
    row = lax.broadcasted_iota(jnp.int32, (half, LANES), 0) % rows
    for part in range(2):
        even = plain[part, pl.ds(0, half, stride=2), :]
        odd = plain[part, pl.ds(1, half, stride=2), :]
        before = jnp.where(row == 0, 0.0, pltpu.roll(odd, 1, 0))
        after = jnp.where(row == rows - 1, 0.0, pltpu.roll(even, half - 1, 0))
        for u, values in enumerate((before, even, odd, after)):
            windows[u, part, :, 1 : breadth + 1] = values.reshape(frames, breadth, rows, LANES)
    chunks = []
    for u in range(4):
        for v in range(4):
            for part in range(2):
                chunks.append(
                    jnp.concatenate(
                        [
                            windows[u, part, frame, pl.ds(v, columns, stride=2)].reshape(
                                columns * rows, LANES
                            )
                            for frame in range(frames)
                        ],
                        axis=0,
                    ).astype(jnp.bfloat16)
                )
    outs = lax.dot_general(
        jnp.concatenate(chunks, axis=1),
        jnp.concatenate([wide_ref[window] for window in range(16)], axis=1),
        NT,
        preferred_element_type=jnp.float32,
    )
    spots = columns * rows

    def from_frame(frame, tap):
        return outs[frame * spots : (frame + 1) * spots, tap * width : (tap + 1) * width]

    def gathered(frame, sources):
        total = jnp.zeros((spots, width), jnp.float32)
        for tap in range(3):
            source = frame + tap - 2
            if source in sources:
                kept = same_clip(clips_ref, jnp.minimum(first + frame, clips_ref.shape[0] - 1), 2 - tap)
                total = total + jnp.where(kept, from_frame(source, tap), 0.0)
        return total

    own = range(frames)
    parts = [
        jnp.concatenate([gathered(frame + ahead, own) for frame in own], axis=1)
        for ahead in (0, frames)
    ]
    parts_out[...] = jnp.concatenate(parts, axis=0).astype(jnp.bfloat16)


def image_scratch(frames, breadth, height):
    return [pltpu.VMEM((3, frames + 1, breadth + 2, height, LANES), jnp.bfloat16)] * 3


def embed_kernel(place_ref, embed_ref, scale_ref, shift_ref, *rest):
    *patch_refs, out_ref = rest
    width = embed_ref.shape[0]
    tokens = out_ref.shape[0]
    total = jnp.zeros((LANES, tokens), jnp.float32)
    begin = 0
    for patch_ref in patch_refs:
        count = patch_ref.shape[0]
        spots = lax.broadcasted_iota(jnp.int32, (count, tokens), 0) + begin
        chosen = (spots == place_ref[0:1, :]) | (spots == place_ref[1:2, :])
        chosen = jnp.where(chosen, 1.0, 0.0).astype(jnp.bfloat16)
        total = total + lax.dot_general(
            patch_ref[...], chosen, TN, preferred_element_type=jnp.float32
        )
        begin += count
    ordered = jnp.where(place_ref[2:3, :] == 0, total[:width], total[width:]).astype(jnp.bfloat16)
    embedded = lax.dot_general(ordered, embed_ref[...], TN, preferred_element_type=jnp.float32)
    center = jnp.mean(embedded, axis=-1, keepdims=True)
    centered = embedded - center
    variance = jnp.mean(centered * centered, axis=-1, keepdims=True)
    normed = centered * lax.rsqrt(variance + 1e-06)
    out_ref[...] = (normed * (1.0 + scale_ref[...]) + shift_ref[...]).astype(out_ref.dtype)


def along_line(unit):
    return [unit] + [xor_permute(unit, "ctx", 4 * step) for step in (1, 2, 3)]


def round_square(half_line):
    return xor_permute(half_line, "ctx", 2), xor_permute(half_line, "groups", 1)


def in_unit_order(low, high, across, other, corners):
    return [low, high, *across, *other, *corners]


def both_cores(pieces):
    return list(pieces) + [xor_permute(piece, "ctx", 1) for piece in pieces]


def unit_channel_map(grid, group, device, unit_channels, units):
    unit = jnp.arange(units * SUBLANES, dtype=jnp.int32) // SUBLANES
    within = jnp.arange(units * SUBLANES, dtype=jnp.int32) % SUBLANES
    if grid:
        step, kind, core = unit % 4, unit // 4 % 4, unit // 16
        source = device ^ (4 * step + 2 * (kind % 2) + core)
        unit = source * 2 + (group ^ (kind // 2))
    return jnp.where(within < unit_channels, unit * unit_channels + within, -1)


def body(
    features,
    clip_ids,
    gain_first,
    weight_first,
    gain_second,
    weight_second,
    gain_third,
    weight_out,
    embed_weight,
    shift_mod,
    scale_mod,
    token_order,
):
    frames, height, breadth, channels = features.shape
    taps = weight_first.shape[0]
    groups, devices = lax.axis_size("groups"), lax.axis_size("ctx")
    group, device = lax.axis_index("groups"), lax.axis_index("ctx")
    grid = groups == 2 and devices == 16
    units = 32
    unit_channels = channels // units
    unpack = functools.partial(unpack_units, taps=taps, unit_channels=unit_channels)

    by_output = [weight.transpose(2, 0, 1) for weight in (weight_first, weight_second)]
    channel_map = unit_channel_map(grid, group, device, unit_channels, units)
    pick = (channel_map[:, None] == jnp.arange(channels, dtype=jnp.int32)).astype(jnp.bfloat16)
    wide = expand_weight_out(weight_out.transpose(0, 2, 1))
    turned = features.transpose(0, 2, 1, 3)
    turned_rim = to_next(features[frames - 2 :], "ctx").transpose(0, 2, 1, 3)

    spots = (height // 2) * (breadth // 2)
    frame, spot = token_order // spots, token_order % spots
    spot = spot % (breadth // 2) * (height // 2) + spot // (breadth // 2)
    owner = frame // frames

    def piece_of(source):
        if not grid:
            return source
        away = source ^ device
        return (away % 2 * 2 + away // 2 % 2) * 4 + away // 4

    own_place = piece_of(owner) * 2 * spots + spot
    sent_place = jnp.where(owner > 0, (piece_of(jnp.maximum(owner - 1, 0)) * 2 + 1) * spots + spot, -1)
    place = jnp.stack([own_place, sent_place, frame % frames])

    if grid:
        half = group.astype(jnp.int32).reshape(1)
        line = along_line(pack_units(half, by_output, unit_channels))
        lows = [jnp.stack([part[index] for part in line[:2]]) for index in range(2)]
        low_squares = round_square(lows[0])
        line, wide, pick, place, turned = lax.optimization_barrier(
            (line, wide, pick, place, turned)
        )
        highs = [jnp.stack([part[index] for part in line[2:]]) for index in range(2)]
        high_squares = round_square(highs[0])
        across, other = zip(low_squares, high_squares)
        corners = xor_permute(other[0], "ctx", 2), xor_permute(across[1], "groups", 1)
        lows, highs, corners, turned_rim = lax.optimization_barrier(
            (lows, highs, corners, turned_rim)
        )
        units_first = both_cores(in_unit_order(lows[0], highs[0], across, other, corners))
        across, other = zip(round_square(lows[1]), round_square(highs[1]))
        corners = xor_permute(other[0], "ctx", 2), xor_permute(across[1], "groups", 1)
        units_second = in_unit_order(lows[1], highs[1], across, other, corners)
    else:
        units_first, units_second = [
            [pack_whole(lax.all_gather(weight, "ctx", axis=0, tiled=True), units)]
            for weight in by_output
        ]

    first = (device * frames).astype(jnp.int32).reshape(1)
    image = pltpu.VMEM((frames, breadth, height, channels), jnp.bfloat16)
    second_in, sent = pl.pallas_call(
        functools.partial(first_kernel, taps=taps, unit_channels=unit_channels),
        out_shape=[image, pltpu.VMEM((3, breadth * height, LANES), jnp.bfloat16)],
        in_specs=[SMEM_SPEC] * 2 + [VMEM_SPEC] * (5 + len(units_first)),
        out_specs=[VMEM_SPEC] * 2,
        scratch_shapes=image_scratch(frames + 2, breadth, height)
        + [
            pltpu.VMEM((taps + (taps + 1) // 2, units * SUBLANES, LANES), jnp.bfloat16),
            pltpu.VMEM((2, SCRATCH_ROWS, LANES), jnp.float32),
        ],
        compiler_params=LARGE,
    )(
        clip_ids, first, IN_VMEM(turned), IN_HBM(turned_rim), gain_first.reshape(1, -1),
        gain_second.reshape(1, -1), IN_VMEM(pick), *map(IN_HBM, units_first),
    )
    second_rim = to_next(sent, "ctx")
    units_second, second_in = lax.optimization_barrier((units_second, second_in))
    rhs_second = [unpack(units_second)]
    if grid:
        rhs_second = both_cores(rhs_second)

    depth = weight_out.shape[2]
    summed = pl.pallas_call(
        functools.partial(own_kernel, taps=taps),
        out_shape=pltpu.VMEM((frames * breadth * height, units * SUBLANES), jnp.float32),
        in_specs=[SMEM_SPEC] * 2 + [VMEM_SPEC] * (3 + len(rhs_second)),
        out_specs=VMEM_SPEC,
        scratch_shapes=image_scratch(frames, breadth, height),
        compiler_params=LARGE,
    )(
        clip_ids, first, IN_VMEM(second_in), IN_VMEM(turned), IN_VMEM(pick),
        *map(IN_VMEM, rhs_second),
    )
    parts = pl.pallas_call(
        functools.partial(second_kernel, taps=taps),
        out_shape=pltpu.VMEM((2 * spots, frames * 4 * depth), jnp.bfloat16),
        in_specs=[SMEM_SPEC] * 2 + [VMEM_SPEC] * (5 + len(rhs_second)),
        out_specs=VMEM_SPEC,
        scratch_shapes=image_scratch(2, breadth, height)
        + [
            pltpu.VMEM((2, frames * breadth * height, LANES), jnp.float32),
            pltpu.VMEM((4, 2, frames, breadth + 2, height // 2, LANES), jnp.float32),
        ],
        compiler_params=LARGE,
    )(
        clip_ids, first, IN_VMEM(second_rim), gain_third.reshape(1, -1), IN_VMEM(pick),
        IN_VMEM(wide), IN_VMEM(summed), *map(IN_VMEM, rhs_second),
    )
    if grid:
        line = jnp.concatenate(along_line(parts))
        pieces = both_cores((line, xor_permute(line, "ctx", 2)))
    else:
        pieces = [lax.all_gather(parts, "ctx", axis=0, tiled=True)]

    tokens, width = token_order.shape[0], embed_weight.shape[1]
    return pl.pallas_call(
        embed_kernel,
        out_shape=jax.ShapeDtypeStruct((tokens, width), jnp.bfloat16),
        in_specs=[VMEM_SPEC] * (4 + len(pieces)),
        out_specs=VMEM_SPEC,
        compiler_params=LARGE,
    )(
        IN_VMEM(place), IN_VMEM(embed_weight), scale_mod.reshape(1, -1), shift_mod.reshape(1, -1),
        *map(IN_VMEM, pieces),
    )


def solution(mesh):
    in_specs = (
        P(("groups", "ctx"), None, None, None),
        P("groups"),
        P(),
        P(None, None, "ctx"),
        P(),
        P(None, None, "ctx"),
        P(),
        P(),
        P(),
        P(),
        P(),
        P(("groups", "ctx")),
    )
    out_specs = P(("groups", "ctx"), None)
    return jax.shard_map(body, mesh=mesh, in_specs=in_specs, out_specs=out_specs, check_vma=False)
```

```python
import functools

import jax
import jax.numpy as jnp
from jax import lax
from jax.experimental import pallas as pl
from jax.experimental.pallas import tpu as pltpu
from jax.sharding import PartitionSpec as P

LANES = 128
SUBLANES = 8
UNIT_ROWS = 256
SCRATCH_ROWS = 304
NT = (((1,), (1,)), ((), ()))
TN = (((0,), (0,)), ((), ()))
VMEM_SPEC = pl.BlockSpec(memory_space=pltpu.VMEM)
SMEM_SPEC = pl.BlockSpec(memory_space=pltpu.SMEM)
IN_VMEM = functools.partial(pltpu.with_memory_space_constraint, memory_space=pltpu.VMEM)
IN_HBM = functools.partial(pltpu.with_memory_space_constraint, memory_space=pltpu.HBM)
SMALL = pltpu.CompilerParams(vmem_limit_bytes=4 * 2**20)
LARGE = pltpu.CompilerParams(vmem_limit_bytes=24 * 2**20)


def xor_permute(value, axis, mask):
    count = lax.axis_size(axis)
    return lax.ppermute(value, axis, [(source, source ^ mask) for source in range(count)])


def to_next(value, axis):
    count = lax.axis_size(axis)
    return lax.ppermute(value, axis, [(source, source + 1) for source in range(count - 1)])


def unit_geometry(taps, unit_channels):
    pairs = (taps + 1) // 2
    head_rows = -(-unit_channels * taps // SUBLANES) * SUBLANES
    return pairs, head_rows


def pack_kernel(half_ref, *refs, unit_channels):
    *weight_refs, unit_ref, staged = refs
    for index, weight_ref in enumerate(weight_refs):
        _, taps, channels = weight_ref.shape
        pairs, head_rows = unit_geometry(taps, unit_channels)
        tail = channels - LANES
        staged[...] = jnp.zeros_like(staged)
        for channel in range(unit_channels):
            rows = weight_ref[half_ref[0] * unit_channels + channel].astype(jnp.float32)
            staged[channel * taps : channel * taps + taps, :] = rows[:, :LANES]
            at = head_rows + channel * pairs
            staged[at : at + pairs, 0:tail] = rows[:pairs, LANES:]
            staged[at : at + taps - pairs, tail : 2 * tail] = rows[pairs:, LANES:]
        unit_ref[index] = staged[...].astype(jnp.bfloat16)


def pack_units(half, weights, unit_channels):
    return pl.pallas_call(
        functools.partial(pack_kernel, unit_channels=unit_channels),
        out_shape=pltpu.VMEM((len(weights), UNIT_ROWS, LANES), jnp.bfloat16),
        in_specs=[SMEM_SPEC] + [VMEM_SPEC] * len(weights),
        out_specs=VMEM_SPEC,
        scratch_shapes=[pltpu.VMEM((UNIT_ROWS, LANES), jnp.float32)],
        compiler_params=SMALL,
    )(half, *map(IN_HBM, weights))


def pack_whole(weight, units):
    outputs, taps, channels = weight.shape
    unit_channels = outputs // units
    pairs, head_rows = unit_geometry(taps, unit_channels)
    split = weight.reshape(units, unit_channels, taps, channels)
    head = split[..., :LANES].reshape(units, unit_channels * taps, LANES)
    head = jnp.pad(head, ((0, 0), (0, head_rows - unit_channels * taps), (0, 0)))
    low, high = split[:, :, :pairs, LANES:], split[:, :, pairs:, LANES:]
    high = jnp.pad(high, ((0, 0), (0, 0), (0, 2 * pairs - taps), (0, 0)))
    tail = jnp.concatenate([low, high], axis=-1).reshape(units, unit_channels * pairs, LANES)
    both = jnp.concatenate([head, tail], axis=1)
    return jnp.pad(both, ((0, 0), (0, UNIT_ROWS - both.shape[1]), (0, 0)))


def expand_kernel(weight_ref, wide_ref):
    depth, channels = weight_ref.shape[1:]
    wide_ref[...] = jnp.zeros_like(wide_ref)
    for u in range(4):
        for v in range(4):
            for a in range(3):
                for r in range(2):
                    for s in range(2):
                        if 0 <= u - r <= 2 and 0 <= v - s <= 2:
                            at = ((a * 2 + r) * 2 + s) * depth
                            wide_ref[4 * u + v, at : at + depth, :channels] = weight_ref[
                                9 * a + 3 * (u - r) + (v - s)
                            ]


def expand_weight_out(weight):
    _, depth, channels = weight.shape
    return pl.pallas_call(
        expand_kernel,
        out_shape=pltpu.VMEM((16, 12 * depth, 2 * LANES), jnp.bfloat16),
        in_specs=[VMEM_SPEC],
        out_specs=VMEM_SPEC,
        compiler_params=SMALL,
    )(IN_HBM(weight))


def rms_silu(values, gain_vector):
    normed = (
        values * lax.rsqrt(jnp.mean(values * values, axis=-1, keepdims=True) + 1e-06) * gain_vector
    )
    return jax.nn.silu(normed)


def same_clip(clips_ref, frame, steps_back):
    earlier = jnp.maximum(frame - steps_back, 0)
    return (frame >= steps_back) & (clips_ref[earlier] == clips_ref[frame])


def split_lanes(values):
    tail = values[:, LANES:]
    fill = jnp.zeros((values.shape[0], 2 * LANES - values.shape[1]), values.dtype)
    return values[:, :LANES], jnp.concatenate([tail, fill], axis=1)


def place_frame(head, tail, at, head_x, low_x, high_x):
    breadth, height = head_x.shape[2] - 2, head_x.shape[3]
    row = lax.broadcasted_iota(jnp.int32, head.shape, 0) % height
    count = head.shape[0]
    for tap in range(3):
        for part, part_x in ((head, head_x), (tail, low_x)):
            if tap == 0:
                part = jnp.where(row == 0, 0.0, pltpu.roll(part, 1, 0))
            if tap == 2:
                part = jnp.where(row == height - 1, 0.0, pltpu.roll(part, count - 1, 0))
            part_x[tap, at, 1 : breadth + 1] = part.reshape(breadth, height, LANES).astype(
                jnp.bfloat16
            )
            if part_x is low_x:
                high_x[tap, at, 1 : breadth + 1] = (
                    pltpu.roll(part, LANES // 2, 1).reshape(breadth, height, LANES)
                ).astype(jnp.bfloat16)


def clear_rims(arrays):
    for array in arrays:
        frames, wide = array.shape[1], array.shape[2]
        array[:, frames - 1] = jnp.zeros_like(array[:, frames - 1])
        array[:, :, 0] = jnp.zeros_like(array[:, :, 0])
        array[:, :, wide - 1] = jnp.zeros_like(array[:, :, wide - 1])


def unpack_kernel(*refs, taps, unit_channels):
    *unit_refs, rhs, staged = refs
    pairs, head_rows = unit_geometry(taps, unit_channels)
    staged[:, UNIT_ROWS:] = jnp.zeros_like(staged[:, UNIT_ROWS:])
    done = 0
    for unit_ref in unit_refs:
        couples = unit_ref.shape[0] // 2

        def couple_step(couple, carry, unit_ref=unit_ref, done=done):
            for one in range(2):
                staged[one, :UNIT_ROWS] = unit_ref[2 * couple + one].astype(jnp.float32)
            to = pl.ds(pl.multiple_of((done + couple) * 16, 16), 16)
            for tap in range(taps):
                rows = [staged[one, pl.ds(tap, 8, stride=taps), :] for one in range(2)]
                rhs[tap, to, :] = jnp.concatenate(rows, axis=0).astype(jnp.bfloat16)
            for pair in range(pairs):
                rows = [staged[one, pl.ds(head_rows + pair, 8, stride=pairs), :] for one in range(2)]
                rhs[taps + pair, to, :] = jnp.concatenate(rows, axis=0).astype(jnp.bfloat16)
            return carry

        lax.fori_loop(0, couples, couple_step, 0)
        done += couples


def unpack_units(pieces, taps, unit_channels, keep=IN_HBM):
    count = sum(piece.shape[0] for piece in pieces)
    return pl.pallas_call(
        functools.partial(unpack_kernel, taps=taps, unit_channels=unit_channels),
        out_shape=pltpu.VMEM((taps + (taps + 1) // 2, count * SUBLANES, LANES), jnp.bfloat16),
        in_specs=[VMEM_SPEC] * len(pieces),
        out_specs=VMEM_SPEC,
        scratch_shapes=[pltpu.VMEM((2, SCRATCH_ROWS, LANES), jnp.float32)],
        compiler_params=SMALL,
    )(*map(keep, pieces))


def convolve(clips_ref, first, frame, held, head_x, low_x, high_x, rhs_refs, taps):
    empty = head_x.shape[1] - 1
    breadth, height = head_x.shape[2] - 2, head_x.shape[3]
    pairs = (taps + 1) // 2
    sources = [
        jnp.where(same_clip(clips_ref, first + frame, 2 - tap), frame + tap - held[0], empty)
        for tap in range(3)
    ]

    def here(tap):
        return tap < taps and frame + tap // 9 in held

    def shifted(array, tap):
        a, b, e = tap // 9, tap // 3 % 3, tap % 3
        return array[b, sources[a], e : e + breadth].reshape(breadth * height, LANES)

    chunks = [(shifted(head_x, tap), tap) for tap in range(taps) if here(tap)]
    for pair in range(pairs):
        parts = []
        if here(pair):
            parts.append(shifted(low_x, pair))
        if here(pair + pairs):
            parts.append(shifted(high_x, pair + pairs))
        if parts:
            chunks.append((sum(parts[1:], parts[0]), taps + pair))
    summed = None
    for begin in range(0, len(chunks), 14):
        group = chunks[begin : begin + 14]
        part = lax.dot_general(
            jnp.concatenate([values for values, _ in group], axis=1),
            jnp.concatenate(
                [jnp.concatenate([rhs[index] for _, index in group], axis=1) for rhs in rhs_refs],
                axis=0,
            ),
            NT,
            preferred_element_type=jnp.float32,
        )
        summed = part if summed is None else summed + part
    return summed


def first_kernel(
    clips_ref, first_ref, own_ref, rim_ref, gain_first_ref, gain_second_ref, pick_ref, *rest,
    taps, unit_channels,
):
    *unit_refs, out_ref, sent_ref, head_x, low_x, high_x, rhs, staged = rest
    frames, breadth, height, channels = own_ref.shape
    clear_rims((head_x, low_x, high_x))
    for frame in range(frames + 2):
        values = rim_ref[frame] if frame < 2 else own_ref[frame - 2]
        values = values.astype(jnp.float32).reshape(breadth * height, channels)
        values = split_lanes(rms_silu(values, gain_first_ref[...]))
        place_frame(*values, frame, head_x, low_x, high_x)
    unpack_kernel(*unit_refs, rhs, staged, taps=taps, unit_channels=unit_channels)
    held = range(frames + 2)
    summed = jnp.concatenate(
        [
            convolve(clips_ref, first_ref[0], frame, held, head_x, low_x, high_x, [rhs], taps)
            for frame in range(frames)
        ],
        axis=0,
    )
    first_out = jnp.dot(
        summed.astype(jnp.bfloat16), pick_ref[...], preferred_element_type=jnp.float32
    )
    second_in = rms_silu(first_out, gain_second_ref[...])
    out_ref[...] = second_in.astype(jnp.bfloat16).reshape(frames, breadth, height, channels)
    pixels = breadth * height
    last = [second_in[at * pixels : (at + 1) * pixels] for at in (frames - 2, frames - 1)]
    sent_ref[0] = last[0][:, :LANES].astype(jnp.bfloat16)
    sent_ref[1] = last[1][:, :LANES].astype(jnp.bfloat16)
    tails = jnp.concatenate([values[:, LANES:] for values in last], axis=1)
    sent_ref[2] = tails.astype(jnp.bfloat16)


def own_kernel(
    clips_ref, first_ref, own_ref, features_ref, pick_ref, *rest, taps
):
    *rhs, summed_ref, head_x, low_x, high_x = rest
    frames, breadth, height, channels = own_ref.shape
    pixels = breadth * height
    clear_rims((head_x, low_x, high_x))
    for frame in range(frames):
        values = own_ref[frame].astype(jnp.float32).reshape(pixels, channels)
        place_frame(*split_lanes(values), frame, head_x, low_x, high_x)
    held = range(2, frames + 2)
    for frame in range(frames):
        features = lax.dot_general(
            features_ref[frame].reshape(pixels, channels),
            pick_ref[...],
            NT,
            preferred_element_type=jnp.float32,
        )
        summed_ref[frame * pixels : (frame + 1) * pixels] = features + convolve(
            clips_ref, first_ref[0], frame, held, head_x, low_x, high_x, rhs, taps
        )


def second_kernel(
    clips_ref, first_ref, rim_ref, gain_ref, pick_ref, wide_ref, summed_ref, *rest, taps
):
    *rhs, parts_out, head_x, low_x, high_x, plain, windows = rest
    breadth, height = head_x.shape[2] - 2, head_x.shape[3]
    pixels = breadth * height
    frames = summed_ref.shape[0] // pixels
    rows, columns = height // 2, breadth // 2
    width = wide_ref.shape[1] // 3
    first = first_ref[0]
    clear_rims((head_x, low_x, high_x))
    for frame in range(2):
        tail = rim_ref[2].astype(jnp.float32)
        if frame == 1:
            tail = pltpu.roll(tail, LANES // 2, 1)
        lane = lax.broadcasted_iota(jnp.int32, tail.shape, 1)
        tail = jnp.where(lane < LANES // 2, tail, 0.0)
        place_frame(rim_ref[frame].astype(jnp.float32), tail, frame, head_x, low_x, high_x)
    sums = []
    for frame in range(frames):
        total = summed_ref[frame * pixels : (frame + 1) * pixels]
        if frame < 2:
            total = total + convolve(
                clips_ref, first, frame, range(2), head_x, low_x, high_x, rhs, taps
            )
        sums.append(total.astype(jnp.bfloat16))
    block_out = jnp.dot(
        jnp.concatenate(sums, axis=0), pick_ref[...], preferred_element_type=jnp.float32
    )
    head_in = rms_silu(block_out, gain_ref[...])
    for part, values in enumerate(split_lanes(head_in)):
        plain[part, : frames * pixels] = values
    for at in (0, breadth + 1):
        windows[:, :, :, at] = jnp.zeros_like(windows[:, :, :, at])
    half = frames * pixels // 2
    row = lax.broadcasted_iota(jnp.int32, (half, LANES), 0) % rows
    for part in range(2):
        even = plain[part, pl.ds(0, half, stride=2), :]
        odd = plain[part, pl.ds(1, half, stride=2), :]
        before = jnp.where(row == 0, 0.0, pltpu.roll(odd, 1, 0))
        after = jnp.where(row == rows - 1, 0.0, pltpu.roll(even, half - 1, 0))
        for u, values in enumerate((before, even, odd, after)):
            windows[u, part, :, 1 : breadth + 1] = values.reshape(frames, breadth, rows, LANES)
    chunks = []
    for u in range(4):
        for v in range(4):
            for part in range(2):
                chunks.append(
                    jnp.concatenate(
                        [
                            windows[u, part, frame, pl.ds(v, columns, stride=2)].reshape(
                                columns * rows, LANES
                            )
                            for frame in range(frames)
                        ],
                        axis=0,
                    ).astype(jnp.bfloat16)
                )
    outs = lax.dot_general(
        jnp.concatenate(chunks, axis=1),
        jnp.concatenate([wide_ref[window] for window in range(16)], axis=1),
        NT,
        preferred_element_type=jnp.float32,
    )
    spots = columns * rows

    def from_frame(frame, tap):
        return outs[frame * spots : (frame + 1) * spots, tap * width : (tap + 1) * width]

    def gathered(frame, sources):
        total = jnp.zeros((spots, width), jnp.float32)
        for tap in range(3):
            source = frame + tap - 2
            if source in sources:
                kept = same_clip(clips_ref, jnp.minimum(first + frame, clips_ref.shape[0] - 1), 2 - tap)
                total = total + jnp.where(kept, from_frame(source, tap), 0.0)
        return total

    own = range(frames)
    parts = [
        jnp.concatenate([gathered(frame + ahead, own) for frame in own], axis=1)
        for ahead in (0, frames)
    ]
    parts_out[...] = jnp.concatenate(parts, axis=0).astype(jnp.bfloat16)


def image_scratch(frames, breadth, height):
    return [pltpu.VMEM((3, frames + 1, breadth + 2, height, LANES), jnp.bfloat16)] * 3


def embed_kernel(place_ref, embed_ref, scale_ref, shift_ref, *rest):
    *patch_refs, out_ref = rest
    width = embed_ref.shape[0]
    tokens = out_ref.shape[0]
    total = jnp.zeros((LANES, tokens), jnp.float32)
    begin = 0
    for patch_ref in patch_refs:
        count = patch_ref.shape[0]
        spots = lax.broadcasted_iota(jnp.int32, (count, tokens), 0) + begin
        chosen = (spots == place_ref[0:1, :]) | (spots == place_ref[1:2, :])
        chosen = jnp.where(chosen, 1.0, 0.0).astype(jnp.bfloat16)
        total = total + lax.dot_general(
            patch_ref[...], chosen, TN, preferred_element_type=jnp.float32
        )
        begin += count
    ordered = jnp.where(place_ref[2:3, :] == 0, total[:width], total[width:]).astype(jnp.bfloat16)
    embedded = lax.dot_general(ordered, embed_ref[...], TN, preferred_element_type=jnp.float32)
    center = jnp.mean(embedded, axis=-1, keepdims=True)
    centered = embedded - center
    variance = jnp.mean(centered * centered, axis=-1, keepdims=True)
    normed = centered * lax.rsqrt(variance + 1e-06)
    out_ref[...] = (normed * (1.0 + scale_ref[...]) + shift_ref[...]).astype(out_ref.dtype)


def along_line(unit):
    return [unit] + [xor_permute(unit, "ctx", 4 * step) for step in (1, 2, 3)]


def round_square(half_line):
    return xor_permute(half_line, "ctx", 2), xor_permute(half_line, "groups", 1)


def in_unit_order(low, high, across, other, corners):
    return [low, high, *across, *other, *corners]


def both_cores(pieces):
    return list(pieces) + [xor_permute(piece, "ctx", 1) for piece in pieces]


def unit_channel_map(grid, group, device, unit_channels, units):
    unit = jnp.arange(units * SUBLANES, dtype=jnp.int32) // SUBLANES
    within = jnp.arange(units * SUBLANES, dtype=jnp.int32) % SUBLANES
    if grid:
        step, kind, core = unit % 4, unit // 4 % 4, unit // 16
        source = device ^ (4 * step + 2 * (kind % 2) + core)
        unit = source * 2 + (group ^ (kind // 2))
    return jnp.where(within < unit_channels, unit * unit_channels + within, -1)


def body(
    features,
    clip_ids,
    gain_first,
    weight_first,
    gain_second,
    weight_second,
    gain_third,
    weight_out,
    embed_weight,
    shift_mod,
    scale_mod,
    token_order,
):
    frames, height, breadth, channels = features.shape
    taps = weight_first.shape[0]
    groups, devices = lax.axis_size("groups"), lax.axis_size("ctx")
    group, device = lax.axis_index("groups"), lax.axis_index("ctx")
    grid = groups == 2 and devices == 16
    units = 32
    unit_channels = channels // units
    unpack = functools.partial(unpack_units, taps=taps, unit_channels=unit_channels)

    by_output = [weight.transpose(2, 0, 1) for weight in (weight_first, weight_second)]
    channel_map = unit_channel_map(grid, group, device, unit_channels, units)
    pick = (channel_map[:, None] == jnp.arange(channels, dtype=jnp.int32)).astype(jnp.bfloat16)
    wide = expand_weight_out(weight_out.transpose(0, 2, 1))
    turned = features.transpose(0, 2, 1, 3)
    turned_rim = to_next(features[frames - 2 :], "ctx").transpose(0, 2, 1, 3)

    spots = (height // 2) * (breadth // 2)
    frame, spot = token_order // spots, token_order % spots
    spot = spot % (breadth // 2) * (height // 2) + spot // (breadth // 2)
    owner = frame // frames

    def piece_of(source):
        if not grid:
            return source
        away = source ^ device
        return (away % 2 * 2 + away // 2 % 2) * 4 + away // 4

    own_place = piece_of(owner) * 2 * spots + spot
    sent_place = jnp.where(owner > 0, (piece_of(jnp.maximum(owner - 1, 0)) * 2 + 1) * spots + spot, -1)
    place = jnp.stack([own_place, sent_place, frame % frames])

    if grid:
        half = group.astype(jnp.int32).reshape(1)
        line = along_line(pack_units(half, by_output, unit_channels))
        lows = [jnp.stack([part[index] for part in line[:2]]) for index in range(2)]
        low_squares = round_square(lows[0])
        line, wide, pick, place, turned = lax.optimization_barrier(
            (line, wide, pick, place, turned)
        )
        highs = [jnp.stack([part[index] for part in line[2:]]) for index in range(2)]
        high_squares = round_square(highs[0])
        across, other = zip(low_squares, high_squares)
        corners = xor_permute(other[0], "ctx", 2), xor_permute(across[1], "groups", 1)
        lows, highs, corners, turned_rim = lax.optimization_barrier(
            (lows, highs, corners, turned_rim)
        )
        units_first = both_cores(in_unit_order(lows[0], highs[0], across, other, corners))
        across, other = zip(round_square(lows[1]), round_square(highs[1]))
        corners = xor_permute(other[0], "ctx", 2), xor_permute(across[1], "groups", 1)
        units_second = in_unit_order(lows[1], highs[1], across, other, corners)
    else:
        units_first, units_second = [
            [pack_whole(lax.all_gather(weight, "ctx", axis=0, tiled=True), units)]
            for weight in by_output
        ]

    first = (device * frames).astype(jnp.int32).reshape(1)
    image = pltpu.VMEM((frames, breadth, height, channels), jnp.bfloat16)
    second_in, sent = pl.pallas_call(
        functools.partial(first_kernel, taps=taps, unit_channels=unit_channels),
        out_shape=[image, pltpu.VMEM((3, breadth * height, LANES), jnp.bfloat16)],
        in_specs=[SMEM_SPEC] * 2 + [VMEM_SPEC] * (5 + len(units_first)),
        out_specs=[VMEM_SPEC] * 2,
        scratch_shapes=image_scratch(frames + 2, breadth, height)
        + [
            pltpu.VMEM((taps + (taps + 1) // 2, units * SUBLANES, LANES), jnp.bfloat16),
            pltpu.VMEM((2, SCRATCH_ROWS, LANES), jnp.float32),
        ],
        compiler_params=LARGE,
    )(
        clip_ids, first, IN_VMEM(turned), IN_HBM(turned_rim), gain_first.reshape(1, -1),
        gain_second.reshape(1, -1), IN_VMEM(pick), *map(IN_HBM, units_first),
    )
    second_rim = to_next(sent, "ctx")
    units_second, second_in = lax.optimization_barrier((units_second, second_in))
    rhs_second = [unpack(units_second)]
    if grid:
        rhs_second = both_cores(rhs_second)

    depth = weight_out.shape[2]
    summed = pl.pallas_call(
        functools.partial(own_kernel, taps=taps),
        out_shape=pltpu.VMEM((frames * breadth * height, units * SUBLANES), jnp.float32),
        in_specs=[SMEM_SPEC] * 2 + [VMEM_SPEC] * (3 + len(rhs_second)),
        out_specs=VMEM_SPEC,
        scratch_shapes=image_scratch(frames, breadth, height),
        compiler_params=LARGE,
    )(
        clip_ids, first, IN_VMEM(second_in), IN_VMEM(turned), IN_VMEM(pick),
        *map(IN_VMEM, rhs_second),
    )
    parts = pl.pallas_call(
        functools.partial(second_kernel, taps=taps),
        out_shape=pltpu.VMEM((2 * spots, frames * 4 * depth), jnp.bfloat16),
        in_specs=[SMEM_SPEC] * 2 + [VMEM_SPEC] * (5 + len(rhs_second)),
        out_specs=VMEM_SPEC,
        scratch_shapes=image_scratch(2, breadth, height)
        + [
            pltpu.VMEM((2, frames * breadth * height + SUBLANES, LANES), jnp.float32),
            pltpu.VMEM((4, 2, frames, breadth + 4, height // 2, LANES), jnp.float32),
        ],
        compiler_params=LARGE,
    )(
        clip_ids, first, IN_VMEM(second_rim), gain_third.reshape(1, -1), IN_VMEM(pick),
        IN_VMEM(wide), IN_VMEM(summed), *map(IN_VMEM, rhs_second),
    )
    if grid:
        line = jnp.concatenate(along_line(parts))
        pieces = both_cores((line, xor_permute(line, "ctx", 2)))
    else:
        pieces = [lax.all_gather(parts, "ctx", axis=0, tiled=True)]

    tokens, width = token_order.shape[0], embed_weight.shape[1]
    return pl.pallas_call(
        embed_kernel,
        out_shape=jax.ShapeDtypeStruct((tokens, width), jnp.bfloat16),
        in_specs=[VMEM_SPEC] * (4 + len(pieces)),
        out_specs=VMEM_SPEC,
        compiler_params=LARGE,
    )(
        IN_VMEM(place), IN_VMEM(embed_weight), scale_mod.reshape(1, -1), shift_mod.reshape(1, -1),
        *map(IN_VMEM, pieces),
    )


def solution(mesh):
    in_specs = (
        P(("groups", "ctx"), None, None, None),
        P("groups"),
        P(),
        P(None, None, "ctx"),
        P(),
        P(None, None, "ctx"),
        P(),
        P(),
        P(),
        P(),
        P(),
        P(("groups", "ctx")),
    )
    out_specs = P(("groups", "ctx"), None)
    return jax.shard_map(body, mesh=mesh, in_specs=in_specs, out_specs=out_specs, check_vma=False)
```

```python
import functools

import jax
import jax.numpy as jnp
from jax import lax
from jax.experimental import pallas as pl
from jax.experimental.pallas import tpu as pltpu
from jax.sharding import PartitionSpec as P

LANES = 128
SUBLANES = 8
UNIT_ROWS = 256
SCRATCH_ROWS = 304
NT = (((1,), (1,)), ((), ()))
TN = (((0,), (0,)), ((), ()))
VMEM_SPEC = pl.BlockSpec(memory_space=pltpu.VMEM)
SMEM_SPEC = pl.BlockSpec(memory_space=pltpu.SMEM)
IN_VMEM = functools.partial(pltpu.with_memory_space_constraint, memory_space=pltpu.VMEM)
IN_HBM = functools.partial(pltpu.with_memory_space_constraint, memory_space=pltpu.HBM)
SMALL = pltpu.CompilerParams(vmem_limit_bytes=4 * 2**20)
LARGE = pltpu.CompilerParams(vmem_limit_bytes=24 * 2**20)


def xor_permute(value, axis, mask):
    count = lax.axis_size(axis)
    return lax.ppermute(value, axis, [(source, source ^ mask) for source in range(count)])


def to_next(value, axis):
    count = lax.axis_size(axis)
    return lax.ppermute(value, axis, [(source, source + 1) for source in range(count - 1)])


def unit_geometry(taps, unit_channels):
    pairs = (taps + 1) // 2
    head_rows = -(-unit_channels * taps // SUBLANES) * SUBLANES
    return pairs, head_rows


def pack_kernel(half_ref, *refs, unit_channels):
    *weight_refs, unit_ref, staged = refs
    for index, weight_ref in enumerate(weight_refs):
        _, taps, channels = weight_ref.shape
        pairs, head_rows = unit_geometry(taps, unit_channels)
        tail = channels - LANES
        staged[...] = jnp.zeros_like(staged)
        for channel in range(unit_channels):
            rows = weight_ref[half_ref[0] * unit_channels + channel].astype(jnp.float32)
            staged[channel * taps : channel * taps + taps, :] = rows[:, :LANES]
            at = head_rows + channel * pairs
            staged[at : at + pairs, 0:tail] = rows[:pairs, LANES:]
            staged[at : at + taps - pairs, tail : 2 * tail] = rows[pairs:, LANES:]
        unit_ref[index] = staged[...].astype(jnp.bfloat16)


def pack_units(half, weights, unit_channels):
    return pl.pallas_call(
        functools.partial(pack_kernel, unit_channels=unit_channels),
        out_shape=pltpu.VMEM((len(weights), UNIT_ROWS, LANES), jnp.bfloat16),
        in_specs=[SMEM_SPEC] + [VMEM_SPEC] * len(weights),
        out_specs=VMEM_SPEC,
        scratch_shapes=[pltpu.VMEM((UNIT_ROWS, LANES), jnp.float32)],
        compiler_params=SMALL,
    )(half, *map(IN_HBM, weights))


def pack_whole(weight, units):
    outputs, taps, channels = weight.shape
    unit_channels = outputs // units
    pairs, head_rows = unit_geometry(taps, unit_channels)
    split = weight.reshape(units, unit_channels, taps, channels)
    head = split[..., :LANES].reshape(units, unit_channels * taps, LANES)
    head = jnp.pad(head, ((0, 0), (0, head_rows - unit_channels * taps), (0, 0)))
    low, high = split[:, :, :pairs, LANES:], split[:, :, pairs:, LANES:]
    high = jnp.pad(high, ((0, 0), (0, 0), (0, 2 * pairs - taps), (0, 0)))
    tail = jnp.concatenate([low, high], axis=-1).reshape(units, unit_channels * pairs, LANES)
    both = jnp.concatenate([head, tail], axis=1)
    return jnp.pad(both, ((0, 0), (0, UNIT_ROWS - both.shape[1]), (0, 0)))


def expand_kernel(weight_ref, wide_ref):
    depth, channels = weight_ref.shape[1:]
    wide_ref[...] = jnp.zeros_like(wide_ref)
    for u in range(4):
        for v in range(4):
            for a in range(3):
                for r in range(2):
                    for s in range(2):
                        if 0 <= u - r <= 2 and 0 <= v - s <= 2:
                            at = ((a * 2 + r) * 2 + s) * depth
                            wide_ref[4 * u + v, at : at + depth, :channels] = weight_ref[
                                9 * a + 3 * (u - r) + (v - s)
                            ]


def expand_weight_out(weight):
    _, depth, channels = weight.shape
    return pl.pallas_call(
        expand_kernel,
        out_shape=pltpu.VMEM((16, 12 * depth, 2 * LANES), jnp.bfloat16),
        in_specs=[VMEM_SPEC],
        out_specs=VMEM_SPEC,
        compiler_params=SMALL,
    )(IN_HBM(weight))


def rms_silu(values, gain_vector):
    normed = (
        values * lax.rsqrt(jnp.mean(values * values, axis=-1, keepdims=True) + 1e-06) * gain_vector
    )
    return jax.nn.silu(normed)


def same_clip(clips_ref, frame, steps_back):
    earlier = jnp.maximum(frame - steps_back, 0)
    return (frame >= steps_back) & (clips_ref[earlier] == clips_ref[frame])


def split_lanes(values):
    tail = values[:, LANES:]
    fill = jnp.zeros((values.shape[0], 2 * LANES - values.shape[1]), values.dtype)
    return values[:, :LANES], jnp.concatenate([tail, fill], axis=1)


def place_frame(head, tail, at, head_x, low_x, high_x):
    breadth, height = head_x.shape[2] - 2, head_x.shape[3]
    row = lax.broadcasted_iota(jnp.int32, head.shape, 0) % height
    count = head.shape[0]
    for tap in range(3):
        for part, part_x in ((head, head_x), (tail, low_x)):
            if tap == 0:
                part = jnp.where(row == 0, 0.0, pltpu.roll(part, 1, 0))
            if tap == 2:
                part = jnp.where(row == height - 1, 0.0, pltpu.roll(part, count - 1, 0))
            part_x[tap, at, 1 : breadth + 1] = part.reshape(breadth, height, LANES).astype(
                jnp.bfloat16
            )
            if part_x is low_x:
                high_x[tap, at, 1 : breadth + 1] = (
                    pltpu.roll(part, LANES // 2, 1).reshape(breadth, height, LANES)
                ).astype(jnp.bfloat16)


def clear_rims(arrays):
    for array in arrays:
        frames, wide = array.shape[1], array.shape[2]
        array[:, frames - 1] = jnp.zeros_like(array[:, frames - 1])
        array[:, :, 0] = jnp.zeros_like(array[:, :, 0])
        array[:, :, wide - 1] = jnp.zeros_like(array[:, :, wide - 1])


def unpack_kernel(*refs, taps, unit_channels):
    *unit_refs, rhs, staged = refs
    pairs, head_rows = unit_geometry(taps, unit_channels)
    staged[:, UNIT_ROWS:] = jnp.zeros_like(staged[:, UNIT_ROWS:])
    done = 0
    for unit_ref in unit_refs:
        couples = unit_ref.shape[0] // 2

        def couple_step(couple, carry, unit_ref=unit_ref, done=done):
            for one in range(2):
                staged[one, :UNIT_ROWS] = unit_ref[2 * couple + one].astype(jnp.float32)
            to = pl.ds(pl.multiple_of((done + couple) * 16, 16), 16)
            for tap in range(taps):
                rows = [staged[one, pl.ds(tap, 8, stride=taps), :] for one in range(2)]
                rhs[tap, to, :] = jnp.concatenate(rows, axis=0).astype(jnp.bfloat16)
            for pair in range(pairs):
                rows = [staged[one, pl.ds(head_rows + pair, 8, stride=pairs), :] for one in range(2)]
                rhs[taps + pair, to, :] = jnp.concatenate(rows, axis=0).astype(jnp.bfloat16)
            return carry

        lax.fori_loop(0, couples, couple_step, 0)
        done += couples


def unpack_units(pieces, taps, unit_channels, keep=IN_HBM):
    count = sum(piece.shape[0] for piece in pieces)
    return pl.pallas_call(
        functools.partial(unpack_kernel, taps=taps, unit_channels=unit_channels),
        out_shape=pltpu.VMEM((taps + (taps + 1) // 2, count * SUBLANES, LANES), jnp.bfloat16),
        in_specs=[VMEM_SPEC] * len(pieces),
        out_specs=VMEM_SPEC,
        scratch_shapes=[pltpu.VMEM((2, SCRATCH_ROWS, LANES), jnp.float32)],
        compiler_params=SMALL,
    )(*map(keep, pieces))


def convolve(clips_ref, first, frame, held, head_x, low_x, high_x, rhs_refs, taps):
    empty = head_x.shape[1] - 1
    breadth, height = head_x.shape[2] - 2, head_x.shape[3]
    pairs = (taps + 1) // 2
    sources = [
        jnp.where(same_clip(clips_ref, first + frame, 2 - tap), frame + tap - held[0], empty)
        for tap in range(3)
    ]

    def here(tap):
        return tap < taps and frame + tap // 9 in held

    def shifted(array, tap):
        a, b, e = tap // 9, tap // 3 % 3, tap % 3
        return array[b, sources[a], e : e + breadth].reshape(breadth * height, LANES)

    chunks = [(shifted(head_x, tap), tap) for tap in range(taps) if here(tap)]
    for pair in range(pairs):
        parts = []
        if here(pair):
            parts.append(shifted(low_x, pair))
        if here(pair + pairs):
            parts.append(shifted(high_x, pair + pairs))
        if parts:
            chunks.append((sum(parts[1:], parts[0]), taps + pair))
    summed = None
    for begin in range(0, len(chunks), 14):
        group = chunks[begin : begin + 14]
        part = lax.dot_general(
            jnp.concatenate([values for values, _ in group], axis=1),
            jnp.concatenate(
                [jnp.concatenate([rhs[index] for _, index in group], axis=1) for rhs in rhs_refs],
                axis=0,
            ),
            NT,
            preferred_element_type=jnp.float32,
        )
        summed = part if summed is None else summed + part
    return summed


def first_kernel(
    clips_ref, first_ref, own_ref, rim_ref, gain_first_ref, gain_second_ref, pick_ref, *rest,
    taps, unit_channels,
):
    *unit_refs, out_ref, sent_ref, head_x, low_x, high_x, rhs, staged = rest
    frames, breadth, height, channels = own_ref.shape
    clear_rims((head_x, low_x, high_x))
    for frame in range(frames + 2):
        values = rim_ref[frame] if frame < 2 else own_ref[frame - 2]
        values = values.astype(jnp.float32).reshape(breadth * height, channels)
        values = split_lanes(rms_silu(values, gain_first_ref[...]))
        place_frame(*values, frame, head_x, low_x, high_x)
    unpack_kernel(*unit_refs, rhs, staged, taps=taps, unit_channels=unit_channels)
    held = range(frames + 2)
    summed = jnp.concatenate(
        [
            convolve(clips_ref, first_ref[0], frame, held, head_x, low_x, high_x, [rhs], taps)
            for frame in range(frames)
        ],
        axis=0,
    )
    first_out = jnp.dot(
        summed.astype(jnp.bfloat16), pick_ref[...], preferred_element_type=jnp.float32
    )
    second_in = rms_silu(first_out, gain_second_ref[...])
    out_ref[...] = second_in.astype(jnp.bfloat16).reshape(frames, breadth, height, channels)
    pixels = breadth * height
    last = [second_in[at * pixels : (at + 1) * pixels] for at in (frames - 2, frames - 1)]
    sent_ref[0] = last[0][:, :LANES].astype(jnp.bfloat16)
    sent_ref[1] = last[1][:, :LANES].astype(jnp.bfloat16)
    tails = jnp.concatenate([values[:, LANES:] for values in last], axis=1)
    sent_ref[2] = tails.astype(jnp.bfloat16)


def own_kernel(
    clips_ref, first_ref, own_ref, features_ref, pick_ref, *rest, taps
):
    *rhs, summed_ref, head_x, low_x, high_x = rest
    frames, breadth, height, channels = own_ref.shape
    pixels = breadth * height
    clear_rims((head_x, low_x, high_x))
    for frame in range(frames):
        values = own_ref[frame].astype(jnp.float32).reshape(pixels, channels)
        place_frame(*split_lanes(values), frame, head_x, low_x, high_x)
    held = range(2, frames + 2)
    for frame in range(frames):
        features = lax.dot_general(
            features_ref[frame].reshape(pixels, channels),
            pick_ref[...],
            NT,
            preferred_element_type=jnp.float32,
        )
        summed_ref[frame * pixels : (frame + 1) * pixels] = features + convolve(
            clips_ref, first_ref[0], frame, held, head_x, low_x, high_x, rhs, taps
        )


def second_kernel(
    clips_ref, first_ref, rim_ref, gain_ref, pick_ref, wide_ref, summed_ref, *rest, taps
):
    *rhs, parts_out, head_x, low_x, high_x, plain, windows = rest
    breadth, height = head_x.shape[2] - 2, head_x.shape[3]
    pixels = breadth * height
    frames = summed_ref.shape[0] // pixels
    rows, columns = height // 2, breadth // 2
    width = wide_ref.shape[1] // 3
    first = first_ref[0]
    clear_rims((head_x, low_x, high_x))
    for frame in range(2):
        tail = rim_ref[2].astype(jnp.float32)
        if frame == 1:
            tail = pltpu.roll(tail, LANES // 2, 1)
        lane = lax.broadcasted_iota(jnp.int32, tail.shape, 1)
        tail = jnp.where(lane < LANES // 2, tail, 0.0)
        place_frame(rim_ref[frame].astype(jnp.float32), tail, frame, head_x, low_x, high_x)
    sums = []
    for frame in range(frames):
        total = summed_ref[frame * pixels : (frame + 1) * pixels]
        if frame < 2:
            total = total + convolve(
                clips_ref, first, frame, range(2), head_x, low_x, high_x, rhs, taps
            )
        sums.append(total.astype(jnp.bfloat16))
    block_out = jnp.dot(
        jnp.concatenate(sums, axis=0), pick_ref[...], preferred_element_type=jnp.float32
    )
    head_in = rms_silu(block_out, gain_ref[...])
    for part, values in enumerate(split_lanes(head_in)):
        plain[part, : frames * pixels] = values
    for at in (0, breadth + 1):
        windows[:, :, :, at] = jnp.zeros_like(windows[:, :, :, at])
    half = frames * pixels // 2
    row = lax.broadcasted_iota(jnp.int32, (half, LANES), 0) % rows
    for part in range(2):
        even = plain[part, pl.ds(0, half, stride=2), :]
        odd = plain[part, pl.ds(1, half, stride=2), :]
        before = jnp.where(row == 0, 0.0, pltpu.roll(odd, 1, 0))
        after = jnp.where(row == rows - 1, 0.0, pltpu.roll(even, half - 1, 0))
        for u, values in enumerate((before, even, odd, after)):
            windows[u, part, :, 1 : breadth + 1] = values.reshape(frames, breadth, rows, LANES)
    chunks = []
    for u in range(4):
        for v in range(4):
            for part in range(2):
                chunks.append(
                    jnp.concatenate(
                        [
                            windows[u, part, frame, pl.ds(v, columns, stride=2)].reshape(
                                columns * rows, LANES
                            )
                            for frame in range(frames)
                        ],
                        axis=0,
                    ).astype(jnp.bfloat16)
                )
    outs = lax.dot_general(
        jnp.concatenate(chunks, axis=1),
        jnp.concatenate([wide_ref[window] for window in range(16)], axis=1),
        NT,
        preferred_element_type=jnp.float32,
    )
    spots = columns * rows

    def from_frame(frame, tap):
        return outs[frame * spots : (frame + 1) * spots, tap * width : (tap + 1) * width]

    def gathered(frame, sources):
        total = jnp.zeros((spots, width), jnp.float32)
        for tap in range(3):
            source = frame + tap - 2
            if source in sources:
                kept = same_clip(clips_ref, jnp.minimum(first + frame, clips_ref.shape[0] - 1), 2 - tap)
                total = total + jnp.where(kept, from_frame(source, tap), 0.0)
        return total

    own = range(frames)
    parts = [
        jnp.concatenate([gathered(frame + ahead, own) for frame in own], axis=1)
        for ahead in (0, frames)
    ]
    parts_out[...] = jnp.concatenate(parts, axis=0).astype(jnp.bfloat16)


def image_scratch(frames, breadth, height):
    return [pltpu.VMEM((3, frames + 1, breadth + 2, height, LANES), jnp.bfloat16)] * 3


def embed_kernel(place_ref, embed_ref, scale_ref, shift_ref, *rest):
    *patch_refs, out_ref = rest
    width = embed_ref.shape[0]
    tokens = out_ref.shape[0]
    total = jnp.zeros((LANES, tokens), jnp.float32)
    begin = 0
    for patch_ref in patch_refs:
        count = patch_ref.shape[0]
        spots = lax.broadcasted_iota(jnp.int32, (count, tokens), 0) + begin
        chosen = (spots == place_ref[0:1, :]) | (spots == place_ref[1:2, :])
        chosen = jnp.where(chosen, 1.0, 0.0).astype(jnp.bfloat16)
        total = total + lax.dot_general(
            patch_ref[...], chosen, TN, preferred_element_type=jnp.float32
        )
        begin += count
    ordered = jnp.where(place_ref[2:3, :] == 0, total[:width], total[width:]).astype(jnp.bfloat16)
    embedded = lax.dot_general(ordered, embed_ref[...], TN, preferred_element_type=jnp.float32)
    center = jnp.mean(embedded, axis=-1, keepdims=True)
    centered = embedded - center
    variance = jnp.mean(centered * centered, axis=-1, keepdims=True)
    normed = centered * lax.rsqrt(variance + 1e-06)
    out_ref[...] = (normed * (1.0 + scale_ref[...]) + shift_ref[...]).astype(out_ref.dtype)


def along_line(unit):
    return [unit] + [xor_permute(unit, "ctx", 4 * step) for step in (3, 2, 1)][::-1]


def round_square(half_line):
    return xor_permute(half_line, "ctx", 2), xor_permute(half_line, "groups", 1)


def in_unit_order(low, high, across, other, corners):
    return [low, high, *across, *other, *corners]


def both_cores(pieces):
    return list(pieces) + [xor_permute(piece, "ctx", 1) for piece in pieces]


def unit_channel_map(grid, group, device, unit_channels, units):
    unit = jnp.arange(units * SUBLANES, dtype=jnp.int32) // SUBLANES
    within = jnp.arange(units * SUBLANES, dtype=jnp.int32) % SUBLANES
    if grid:
        step, kind, core = unit % 4, unit // 4 % 4, unit // 16
        source = device ^ (4 * step + 2 * (kind % 2) + core)
        unit = source * 2 + (group ^ (kind // 2))
    return jnp.where(within < unit_channels, unit * unit_channels + within, -1)


def body(
    features,
    clip_ids,
    gain_first,
    weight_first,
    gain_second,
    weight_second,
    gain_third,
    weight_out,
    embed_weight,
    shift_mod,
    scale_mod,
    token_order,
):
    frames, height, breadth, channels = features.shape
    taps = weight_first.shape[0]
    groups, devices = lax.axis_size("groups"), lax.axis_size("ctx")
    group, device = lax.axis_index("groups"), lax.axis_index("ctx")
    grid = groups == 2 and devices == 16
    units = 32
    unit_channels = channels // units
    unpack = functools.partial(unpack_units, taps=taps, unit_channels=unit_channels)

    by_output = [weight.transpose(2, 0, 1) for weight in (weight_first, weight_second)]
    channel_map = unit_channel_map(grid, group, device, unit_channels, units)
    pick = (channel_map[:, None] == jnp.arange(channels, dtype=jnp.int32)).astype(jnp.bfloat16)
    wide = expand_weight_out(weight_out.transpose(0, 2, 1))
    turned = features.transpose(0, 2, 1, 3)
    turned_rim = to_next(features[frames - 2 :], "ctx").transpose(0, 2, 1, 3)

    spots = (height // 2) * (breadth // 2)
    frame, spot = token_order // spots, token_order % spots
    spot = spot % (breadth // 2) * (height // 2) + spot // (breadth // 2)
    owner = frame // frames

    def piece_of(source):
        if not grid:
            return source
        away = source ^ device
        return (away % 2 * 2 + away // 2 % 2) * 4 + away // 4

    own_place = piece_of(owner) * 2 * spots + spot
    sent_place = jnp.where(owner > 0, (piece_of(jnp.maximum(owner - 1, 0)) * 2 + 1) * spots + spot, -1)
    place = jnp.stack([own_place, sent_place, frame % frames])

    if grid:
        half = group.astype(jnp.int32).reshape(1)
        line = along_line(pack_units(half, by_output, unit_channels))
        lows = [jnp.stack([part[index] for part in line[:2]]) for index in range(2)]
        low_squares = round_square(lows[0])
        line, wide, pick, place, turned = lax.optimization_barrier(
            (line, wide, pick, place, turned)
        )
        highs = [jnp.stack([part[index] for part in line[2:]]) for index in range(2)]
        high_squares = round_square(highs[0])
        across, other = zip(low_squares, high_squares)
        corners = xor_permute(other[0], "ctx", 2), xor_permute(across[1], "groups", 1)
        lows, highs, corners, turned_rim = lax.optimization_barrier(
            (lows, highs, corners, turned_rim)
        )
        units_first = both_cores(in_unit_order(lows[0], highs[0], across, other, corners))
        across, other = zip(round_square(lows[1]), round_square(highs[1]))
        corners = xor_permute(other[0], "ctx", 2), xor_permute(across[1], "groups", 1)
        units_second = in_unit_order(lows[1], highs[1], across, other, corners)
    else:
        units_first, units_second = [
            [pack_whole(lax.all_gather(weight, "ctx", axis=0, tiled=True), units)]
            for weight in by_output
        ]

    first = (device * frames).astype(jnp.int32).reshape(1)
    image = pltpu.VMEM((frames, breadth, height, channels), jnp.bfloat16)
    second_in, sent = pl.pallas_call(
        functools.partial(first_kernel, taps=taps, unit_channels=unit_channels),
        out_shape=[image, pltpu.VMEM((3, breadth * height, LANES), jnp.bfloat16)],
        in_specs=[SMEM_SPEC] * 2 + [VMEM_SPEC] * (5 + len(units_first)),
        out_specs=[VMEM_SPEC] * 2,
        scratch_shapes=image_scratch(frames + 2, breadth, height)
        + [
            pltpu.VMEM((taps + (taps + 1) // 2, units * SUBLANES, LANES), jnp.bfloat16),
            pltpu.VMEM((2, SCRATCH_ROWS, LANES), jnp.float32),
        ],
        compiler_params=LARGE,
    )(
        clip_ids, first, IN_VMEM(turned), IN_HBM(turned_rim), gain_first.reshape(1, -1),
        gain_second.reshape(1, -1), IN_VMEM(pick), *map(IN_HBM, units_first),
    )
    second_rim = to_next(sent, "ctx")
    units_second, second_in = lax.optimization_barrier((units_second, second_in))
    rhs_second = [unpack(units_second)]
    if grid:
        rhs_second = both_cores(rhs_second)

    depth = weight_out.shape[2]
    summed = pl.pallas_call(
        functools.partial(own_kernel, taps=taps),
        out_shape=pltpu.VMEM((frames * breadth * height, units * SUBLANES), jnp.float32),
        in_specs=[SMEM_SPEC] * 2 + [VMEM_SPEC] * (3 + len(rhs_second)),
        out_specs=VMEM_SPEC,
        scratch_shapes=image_scratch(frames, breadth, height),
        compiler_params=LARGE,
    )(
        clip_ids, first, IN_VMEM(second_in), IN_VMEM(turned), IN_VMEM(pick),
        *map(IN_VMEM, rhs_second),
    )
    parts = pl.pallas_call(
        functools.partial(second_kernel, taps=taps),
        out_shape=pltpu.VMEM((2 * spots, frames * 4 * depth), jnp.bfloat16),
        in_specs=[SMEM_SPEC] * 2 + [VMEM_SPEC] * (5 + len(rhs_second)),
        out_specs=VMEM_SPEC,
        scratch_shapes=image_scratch(2, breadth, height)
        + [
            pltpu.VMEM((2, frames * breadth * height + SUBLANES, LANES), jnp.float32),
            pltpu.VMEM((4, 2, frames, breadth + 4, height // 2, LANES), jnp.float32),
        ],
        compiler_params=LARGE,
    )(
        clip_ids, first, IN_VMEM(second_rim), gain_third.reshape(1, -1), IN_VMEM(pick),
        IN_VMEM(wide), IN_VMEM(summed), *map(IN_VMEM, rhs_second),
    )
    if grid:
        line = jnp.concatenate(along_line(parts))
        pieces = both_cores((line, xor_permute(line, "ctx", 2)))
    else:
        pieces = [lax.all_gather(parts, "ctx", axis=0, tiled=True)]

    tokens, width = token_order.shape[0], embed_weight.shape[1]
    return pl.pallas_call(
        embed_kernel,
        out_shape=jax.ShapeDtypeStruct((tokens, width), jnp.bfloat16),
        in_specs=[VMEM_SPEC] * (4 + len(pieces)),
        out_specs=VMEM_SPEC,
        compiler_params=LARGE,
    )(
        IN_VMEM(place), IN_VMEM(embed_weight), scale_mod.reshape(1, -1), shift_mod.reshape(1, -1),
        *map(IN_VMEM, pieces),
    )


def solution(mesh):
    in_specs = (
        P(("groups", "ctx"), None, None, None),
        P("groups"),
        P(),
        P(None, None, "ctx"),
        P(),
        P(None, None, "ctx"),
        P(),
        P(),
        P(),
        P(),
        P(),
        P(("groups", "ctx")),
    )
    out_specs = P(("groups", "ctx"), None)
    return jax.shard_map(body, mesh=mesh, in_specs=in_specs, out_specs=out_specs, check_vma=False)
```
